32 devices in a mesh: occ: 2 (over core), aux: 16 (over z, y, x).
Axes of the slice: x: 2, y: 2, z: 4, core: 2. Of those that a mesh axis runs over, the one named last changes fastest.
Arguments:
- coeffs: bfloat16 [2, 256, 65536], P('occ', None, 'aux'), may hold values from -0.375 to 0.375
- occ_energy: bfloat16 [2], P('occ'), may hold values from -1.5 to -0.29882812
- virt_energy: bfloat16 [256], replicated, may hold values from 0.19921875 to 3
- screen: int32 [2, 512], P('occ', 'aux'), may hold values 0 or 1
- owner: int32 [512], P('aux'), may hold values from 0 to 127
- positions: float32 [3, 128], replicated, may hold values from -1 to 1
Outputs:
- gamma: bfloat16 [2, 256, 65536], P('occ', None, 'aux')
- virial: float32 [9, 65536], P(None, 'aux')
The draws below stay inside these ranges and needn't reach their ends.
All inputs are finite; a program needn't handle non-finite values. No bound on the sum of `screen` on one device may be relied on, other than what follows from the above.
Results may differ from the reference program's by a relative error of at most 0.0049.
Values may be sent and summed in bfloat16 or wider, within the bound.
No kernel may reach another device: no remote copies, remote signals or barrier semaphores. Data moves between devices by JAX's collectives and lax.ppermute only.
A program may use at most 64 MiB of HBM per device.

```python
import jax
import jax.numpy as jnp
from jax import lax

OCC_DEV = 1
VIRT = 256
ABLK = 128
ATOMS = 128
NOCC = 2
NAUX = 65536
ABLOCKS = 512
N_OCC = 2


def with_ends(entries, stream_key, smallest, largest):
    longest = entries.shape.index(max(entries.shape))
    spots = []
    for shift in (0, 1):
        where = [jax.random.randint(jax.random.fold_in(stream_key, axis), (), 0, length) for axis, length in enumerate(entries.shape)]
        where[longest] = (where[longest] + shift) % entries.shape[longest]
        spots.append(tuple(where))
    return entries.at[spots[0]].set(smallest).at[spots[1]].set(largest)


def block_scale(stream_key, shape, pieces, least, top_value):
    loudness = 1.0
    for position, parts in pieces:
        heights = jax.random.uniform(jax.random.fold_in(jax.random.fold_in(stream_key, 6), position), (parts,), jnp.float32, least / len(pieces), top_value / len(pieces))
        loudness = loudness * jnp.repeat(jnp.exp(heights), shape[position] // parts).reshape((-1,) + (1,) * (len(shape) - 1 - position))
    return loudness


def bell_draw(stream_key, shape, width, most, pieces=(), kind=jnp.bfloat16):
    loudness = block_scale(stream_key, shape, pieces, -0.22, 0.18) if pieces else 1.0
    array = jax.random.normal(stream_key, shape, jnp.float32) * width * loudness
    return jnp.minimum(jnp.maximum(array, -most), most).astype(kind)


def setup_inputs(seed: int = 0) -> dict:
    arg_keys = jax.random.split(jax.random.key(seed), 7)
    return {
        "coeffs": bell_draw(arg_keys[0], (NOCC, VIRT, NAUX), (NAUX ** -0.25), 0.375, ((0, 2), (2, 16))),
        "occ_energy": jnp.clip(-1.5 + 1.2011719 * jax.random.uniform(arg_keys[1], (NOCC,), jnp.float32) ** block_scale(arg_keys[1], (NOCC,), ((0, 2),), -0.2, 0.2), -1.5, -0.29882812).astype(jnp.bfloat16),
        "virt_energy": jnp.clip(jax.random.uniform(arg_keys[2], (VIRT,), jnp.float32, 0.19921875, 3.0), 0.19921875, 3.0).astype(jnp.bfloat16),
        "screen": with_ends((jax.random.randint(arg_keys[3], (N_OCC, ABLOCKS), 0, 3) < 2).astype(jnp.int32), jax.random.fold_in(arg_keys[3], 1), 0, 1),
        "owner": with_ends(jax.random.randint(arg_keys[4], (ABLOCKS,), 0, ATOMS), jax.random.fold_in(arg_keys[4], 1), 0, ATOMS - 1).astype(jnp.int32),
        "positions": jnp.clip(jax.random.uniform(arg_keys[5], (3, ATOMS), jnp.float32, -1.0, 1.0), -1.0, 1.0),
    }


def reference(coeffs, occ_energy, virt_energy, screen, owner, positions):
    mask = jnp.repeat(jnp.repeat(screen, OCC_DEV, axis=0), ABLK, axis=1).astype(jnp.bfloat16)
    masked = coeffs * mask[:, None, :]
    flat = masked.reshape(NOCC * VIRT, NAUX).astype(jnp.float32)
    pairs = jnp.dot(flat, flat.T, precision=lax.Precision.HIGHEST)
    spread = (virt_energy.astype(jnp.float32)[None, :] - occ_energy.astype(jnp.float32)[:, None]).reshape(-1)
    amps = (pairs / (spread[:, None] + spread[None, :])).astype(jnp.bfloat16)
    gamma = jnp.dot(amps.astype(jnp.float32), flat, precision=lax.Precision.HIGHEST).astype(jnp.bfloat16)
    weight = jnp.sum(gamma.astype(jnp.float32) * flat, axis=0)
    where = jnp.repeat(positions[:, owner], ABLK, axis=1)
    virial = (where[:, None, :] * where[None, :, :]).reshape(9, NAUX) * weight[None, :]
    return gamma.reshape(NOCC, VIRT, NAUX), virial
```

```python
import functools

import jax
import jax.numpy as jnp
from jax import lax
from jax.experimental import pallas as pl
from jax.experimental.pallas import tpu as pltpu
from jax.sharding import PartitionSpec as P

F32 = jnp.float32
BF16 = jnp.bfloat16
CONTRACT_LAST = (((1,), (1,)), ((), ()))
SMEM = pltpu.MemorySpace.SMEM
VMEM = pltpu.MemorySpace.VMEM


def mask_row(screen_ref, first, count, width):
    pieces = [
        jnp.full((1, width), screen_ref[0, first + k].astype(F32), F32) for k in range(count)
    ]
    return jnp.concatenate(pieces, axis=1).astype(BF16)


def own_pairs_kernel(blocks, width, screen_ref, own_ref, sum_ref, send_ref, total):
    step = pl.program_id(0)
    own = own_ref[...]
    mask = mask_row(screen_ref, step * blocks, blocks, width)
    term = lax.dot_general(own * mask, own, CONTRACT_LAST, preferred_element_type=F32)

    @pl.when(step == 0)
    def _():
        total[...] = term

    @pl.when(step > 0)
    def _():
        total[...] += term

    @pl.when(step == pl.num_programs(0) - 1)
    def _():
        half = total.shape[0] // 2
        low, high = pl.ds(0, half), pl.ds(half, half)
        for place, (rows, cols) in enumerate(((low, low), (high, low), (high, high))):
            part = total[rows, cols]
            sum_ref[pl.ds(place * half, half), :] = part
            send_ref[pl.ds(place * half, half), :] = part.astype(BF16)


def cross_pairs_kernel(
    blocks, width, screen_ref, other_screen_ref, own_ref, other_ref, sum_ref, send_ref, total
):
    step = pl.program_id(0)
    core = lax.axis_index("occ")
    mask = mask_row(screen_ref, step * blocks, blocks, width) * mask_row(
        other_screen_ref, step * blocks, blocks, width
    )
    term = lax.dot_general(
        own_ref[...] * mask, other_ref[...], CONTRACT_LAST, preferred_element_type=F32
    )

    @pl.when(step == 0)
    def _():
        total[...] = term

    @pl.when(step > 0)
    def _():
        total[...] += term

    @pl.when(step == pl.num_programs(0) - 1)
    def _():
        half = total.shape[0] // 2
        for place in range(2):
            rows = pl.ds(place * half, half)
            straight = total[rows, pl.ds(place * half, half)]
            across = total[rows, pl.ds((1 - place) * half, half)]
            part = jnp.where(core == 0, straight, across)
            sum_ref[rows, :] = part
            send_ref[rows, :] = part.astype(BF16)


def tiles(aux_dev, blocks):
    steps = 4 if blocks % 4 == 0 else 1
    return steps, aux_dev // steps, blocks // steps


def own_pairs(own, screen):
    virt, aux_dev = own.shape
    blocks = screen.shape[1]
    steps, tile, per_step = tiles(aux_dev, blocks)
    half = virt // 2
    return pl.pallas_call(
        functools.partial(own_pairs_kernel, per_step, aux_dev // blocks),
        grid=(steps,),
        in_specs=[
            pl.BlockSpec(memory_space=SMEM),
            pl.BlockSpec((virt, tile), lambda i: (0, i)),
        ],
        out_specs=[pl.BlockSpec((3 * half, half), lambda i: (0, 0))] * 2,
        out_shape=[
            jax.ShapeDtypeStruct((3 * half, half), F32),
            jax.ShapeDtypeStruct((3 * half, half), BF16),
        ],
        scratch_shapes=[pltpu.VMEM((virt, virt), F32)],
        compiler_params=pltpu.CompilerParams(vmem_limit_bytes=16 << 20),
        cost_estimate=pl.CostEstimate(
            flops=2 * virt * virt * aux_dev, bytes_accessed=2 * virt * aux_dev, transcendentals=0
        ),
        name="own_pairs",
    )(screen, own)


def cross_pairs(own, other, screen, other_screen):
    virt, aux_dev = own.shape
    blocks = screen.shape[1]
    steps, tile, per_step = tiles(aux_dev, blocks)
    half = virt // 2
    return pl.pallas_call(
        functools.partial(cross_pairs_kernel, per_step, aux_dev // blocks),
        grid=(steps,),
        in_specs=[
            pl.BlockSpec(memory_space=SMEM),
            pl.BlockSpec(memory_space=SMEM),
            pl.BlockSpec((virt, tile), lambda i: (0, i)),
            pl.BlockSpec((virt, tile), lambda i: (0, i)),
        ],
        out_specs=[pl.BlockSpec((2 * half, half), lambda i: (0, 0))] * 2,
        out_shape=[
            jax.ShapeDtypeStruct((2 * half, half), F32),
            jax.ShapeDtypeStruct((2 * half, half), BF16),
        ],
        scratch_shapes=[pltpu.VMEM((virt, virt), F32)],
        compiler_params=pltpu.CompilerParams(vmem_limit_bytes=16 << 20),
        cost_estimate=pl.CostEstimate(
            flops=2 * virt * virt * aux_dev, bytes_accessed=4 * virt * aux_dev, transcendentals=0
        ),
        name="cross_pairs",
    )(screen, other_screen, own, other)


def symmetric(packed):
    half = packed.shape[1]
    first, low, last = (packed[k * half : (k + 1) * half, :] for k in range(3))
    top = jnp.concatenate([first, low.T], axis=1)
    return jnp.concatenate([top, jnp.concatenate([low, last], axis=1)], axis=0)


def gamma_kernel(
    blocks,
    width,
    screen_ref,
    other_screen_ref,
    owner_ref,
    positions_ref,
    energy_ref,
    other_energy_ref,
    virt_ref,
    own_sum_ref,
    other_sum_ref,
    cross_sum_ref,
    other_cross_ref,
    own_ref,
    other_ref,
    gamma_ref,
    virial_ref,
    amps,
    other_amps,
):
    step = pl.program_id(0)
    core = lax.axis_index("occ")
    virt = own_ref.shape[0]
    half = virt // 2

    @pl.when(step == 0)
    def _():
        virt_row = jnp.broadcast_to(virt_ref[...].astype(F32), (virt, virt))
        virt_col = virt_row.T
        energy = energy_ref[...].astype(F32)
        other_energy = other_energy_ref[...].astype(F32)
        own_row, own_col = virt_row - energy, virt_col - energy
        other_row, other_col = virt_row - other_energy, virt_col - other_energy
        amps[:, 0:virt] = (symmetric(own_sum_ref[...]) / (own_col + own_row)).astype(BF16)
        other_amps[...] = (symmetric(other_sum_ref[...]) / (other_col + other_row)).astype(BF16)
        mine = [cross_sum_ref[pl.ds(k * half, half), :] for k in range(2)]
        theirs = [other_cross_ref[pl.ds(k * half, half), :].T for k in range(2)]
        even = core == 0
        cross = jnp.concatenate(
            [
                jnp.concatenate(
                    [jnp.where(even, mine[0], theirs[0]), jnp.where(even, theirs[1], mine[0])], axis=1
                ),
                jnp.concatenate(
                    [jnp.where(even, theirs[0], mine[1]), jnp.where(even, mine[1], theirs[1])], axis=1
                ),
            ],
            axis=0,
        )
        amps[:, virt : 2 * virt] = (cross / (own_col + other_row)).astype(BF16)

    own = own_ref[...] * mask_row(screen_ref, step * blocks, blocks, width)
    other = other_ref[...] * mask_row(other_screen_ref, step * blocks, blocks, width)
    cross_part = jnp.dot(amps[:, virt : 2 * virt], other, preferred_element_type=F32)
    gamma = (
        jnp.dot(amps[:, 0:virt], own, preferred_element_type=F32) + cross_part
    ).astype(BF16)
    gamma_ref[...] = gamma
    other_part = jnp.dot(other_amps[...], other, preferred_element_type=F32)
    weight = jnp.sum(
        (gamma.astype(F32) + cross_part) * own.astype(F32) + other_part * other.astype(F32),
        axis=0,
        keepdims=True,
    )
    for k in range(blocks):
        atom = owner_ref[0, step * blocks + k]
        where = [positions_ref[c, atom] for c in range(3)]
        part = weight[:, k * width : (k + 1) * width]
        rows = [part * (where[c] * where[d]) for c in range(3) for d in range(3)]
        virial_ref[:, k * width : (k + 1) * width] = jnp.concatenate(rows, axis=0)


def gamma_and_virial(
    own, other, screen, other_screen, owner, positions, energy, other_energy, virt_energy,
    own_sum, other_sum, cross_sum, other_cross,
):
    virt, aux_dev = own.shape
    blocks = screen.shape[1]
    steps, tile, per_step = tiles(aux_dev, blocks)
    smem = pl.BlockSpec(memory_space=SMEM)
    vmem = pl.BlockSpec(memory_space=VMEM)
    column_block = pl.BlockSpec((virt, tile), lambda i: (0, i))
    return pl.pallas_call(
        functools.partial(gamma_kernel, per_step, aux_dev // blocks),
        grid=(steps,),
        in_specs=[smem] * 4 + [vmem] * 7 + [column_block] * 2,
        out_specs=[column_block, pl.BlockSpec((9, tile), lambda i: (0, i))],
        out_shape=[
            jax.ShapeDtypeStruct((virt, aux_dev), BF16),
            jax.ShapeDtypeStruct((9, aux_dev), F32),
        ],
        scratch_shapes=[pltpu.VMEM((virt, 2 * virt), BF16), pltpu.VMEM((virt, virt), BF16)],
        compiler_params=pltpu.CompilerParams(vmem_limit_bytes=24 << 20),
        cost_estimate=pl.CostEstimate(
            flops=6 * virt * virt * aux_dev, bytes_accessed=6 * virt * aux_dev, transcendentals=0
        ),
        name="gamma_and_virial",
    )(
        screen, other_screen, owner.reshape(1, -1), positions,
        energy.reshape(1, 1), other_energy.reshape(1, 1), virt_energy.reshape(1, -1),
        own_sum, other_sum, cross_sum, other_cross, own, other,
    )


def swap(array, axis, size, bit):
    return lax.ppermute(array, axis, [(i, i ^ bit) for i in range(size)])


def sum_over_aux(total, send, n_aux, bits):
    for bit in bits:
        total = total + swap(send, "aux", n_aux, bit).astype(F32)
        send = total.astype(BF16)
    return total


def two_occ_body(n_aux, coeffs, occ_energy, virt_energy, screen, owner, positions):
    own = coeffs[0]
    other = swap(own, "occ", 2, 1)
    other_screen = swap(screen, "occ", 2, 1)
    other_energy = swap(occ_energy, "occ", 2, 1)
    bits = [1 << k for k in range(n_aux.bit_length() - 1)]
    own_sum, own_send = own_pairs(own, screen)
    cross_sum, cross_send = cross_pairs(own, other, screen, other_screen)
    own_sum = sum_over_aux(own_sum, own_send, n_aux, bits)
    cross_sum = sum_over_aux(cross_sum, cross_send, n_aux, bits)
    other_sum = swap(own_sum, "occ", 2, 1)
    other_cross = swap(cross_sum, "occ", 2, 1)
    gamma, virial = gamma_and_virial(
        own, other, screen, other_screen, owner, positions, occ_energy, other_energy, virt_energy,
        own_sum, other_sum, cross_sum, other_cross,
    )
    return gamma[None], virial


def general_body(n_aux, coeffs, occ_energy, virt_energy, screen, owner, positions):
    occ_dev, virt, aux_dev = coeffs.shape
    width = aux_dev // screen.shape[1]
    column_mask = jnp.repeat(screen[0], width).astype(BF16)
    masked = coeffs * column_mask[None, None, :]
    whole = lax.all_gather(masked, "occ", axis=0, tiled=True)
    energies = lax.all_gather(occ_energy, "occ", axis=0, tiled=True)
    all_rows = whole.reshape(-1, aux_dev)
    local = masked.reshape(-1, aux_dev)
    virt_f = virt_energy.astype(F32)
    spread_local = (virt_f[None, :] - occ_energy.astype(F32)[:, None]).reshape(-1)
    spread_all = (virt_f[None, :] - energies.astype(F32)[:, None]).reshape(-1)
    pairs = lax.dot_general(all_rows, local, CONTRACT_LAST, preferred_element_type=F32)
    if n_aux & (n_aux - 1):
        summed = lax.psum(pairs, "aux")
    else:
        bits = [1 << k for k in range(n_aux.bit_length() - 1)]
        summed = sum_over_aux(pairs, pairs.astype(BF16), n_aux, bits)
    amps = (summed / (spread_all[:, None] + spread_local[None, :])).astype(BF16)
    gamma = lax.dot_general(
        amps, all_rows, (((0,), (0,)), ((), ())), preferred_element_type=F32
    ).astype(BF16)
    partial_weight = jnp.sum(gamma.astype(F32) * local.astype(F32), axis=0)
    weight = lax.psum(partial_weight, "occ")
    where = jnp.repeat(positions[:, owner], width, axis=1)
    virial = (where[:, None, :] * where[None, :, :]).reshape(9, aux_dev) * weight[None, :]
    return gamma.reshape(occ_dev, virt, aux_dev), virial


def solution(mesh):
    placed = (P("occ", None, "aux"), P("occ"), P(), P("occ", "aux"), P("aux"), P())
    n_occ, n_aux = mesh.shape["occ"], mesh.shape["aux"]
    power_of_two = n_aux & (n_aux - 1) == 0

    def body(coeffs, *rest):
        fits = n_occ == 2 and coeffs.shape[0] == 1 and power_of_two
        chosen = two_occ_body if fits else general_body
        return chosen(n_aux, coeffs, *rest)

    return jax.shard_map(
        body,
        mesh=mesh,
        in_specs=placed,
        out_specs=(P("occ", None, "aux"), P(None, "aux")),
        check_vma=False,
    )
```

```python
import functools

import jax
import jax.numpy as jnp
from jax import lax
from jax.experimental import pallas as pl
from jax.experimental.pallas import tpu as pltpu
from jax.sharding import PartitionSpec as P

F32 = jnp.float32
BF16 = jnp.bfloat16
CONTRACT_LAST = (((1,), (1,)), ((), ()))
SMEM = pltpu.MemorySpace.SMEM
VMEM = pltpu.MemorySpace.VMEM
PAD = 16


def mask_row(screen, first, count, width):
    values = screen.astype(F32)
    pieces = [
        jnp.broadcast_to(values[:, k : k + 1], (1, width)) for k in range(first, first + count)
    ]
    return jnp.concatenate(pieces, axis=1).astype(BF16)


def split(aux_dev, blocks, wanted):
    steps = wanted if blocks % wanted == 0 else 1
    return steps, aux_dev // steps, blocks // steps


def triangle(size):
    return (lax.broadcasted_iota(jnp.int32, (size, size), axis) for axis in (0, 1))


def own_pairs_kernel(
    blocks, width, screen_hbm, own_hbm, own_ref, sum_ref, send_ref, total, screen, own_sem, screen_sem
):
    half = total.shape[0] // 2
    screen_copy = pltpu.make_async_copy(screen_hbm, screen, screen_sem)
    own_copy = pltpu.make_async_copy(own_hbm, own_ref, own_sem)
    screen_copy.start()
    own_copy.start()
    screen_copy.wait()
    mask = mask_row(screen[...], 0, blocks, width)
    own_copy.wait()
    own = own_ref[...]
    total[...] = lax.dot_general(own * mask, own, CONTRACT_LAST, preferred_element_type=F32)
    low, high = pl.ds(0, half), pl.ds(half, half)
    row, col = triangle(half)
    first, last = total[low, low], total[high, high]
    diagonal = jnp.sum(jnp.where(row == col, last, 0.0), axis=0, keepdims=True)
    parts = (
        total[high, low],
        jnp.where(row >= col, first, last),
        jnp.broadcast_to(diagonal, (PAD, half)),
    )
    start = 0
    for part in parts:
        rows = pl.ds(start, part.shape[0])
        sum_ref[rows, :] = part
        send_ref[rows, :] = part.astype(BF16)
        start += part.shape[0]


def cross_pairs_kernel(
    blocks, width, screen_ref, other_screen_ref, own_ref, other_ref, sum_ref, send_ref, total
):
    half = total.shape[0] // 2
    core = lax.axis_index("occ")
    mask = mask_row(screen_ref[...] * other_screen_ref[...], 0, blocks, width)
    total[...] = lax.dot_general(
        own_ref[...], other_ref[...] * mask, CONTRACT_LAST, preferred_element_type=F32
    )
    for place in range(2):
        rows = pl.ds(place * half, half)
        straight = total[rows, pl.ds(place * half, half)]
        across = total[rows, pl.ds((1 - place) * half, half)]
        part = jnp.where(core == 0, straight, across)
        sum_ref[rows, :] = part
        send_ref[rows, :] = part.astype(BF16)


def in_hbm(array):
    return pltpu.with_memory_space_constraint(array, pltpu.HBM)


def own_pairs(own, screen):
    virt, aux_dev = own.shape
    blocks = screen.shape[1]
    half = virt // 2
    hbm = pl.BlockSpec(memory_space=pltpu.HBM)
    return pl.pallas_call(
        functools.partial(own_pairs_kernel, blocks, aux_dev // blocks),
        in_specs=[hbm, hbm],
        out_specs=[pl.BlockSpec(memory_space=VMEM)] * 3,
        out_shape=[
            jax.ShapeDtypeStruct((virt, aux_dev), BF16),
            jax.ShapeDtypeStruct((2 * half + PAD, half), F32),
            jax.ShapeDtypeStruct((2 * half + PAD, half), BF16),
        ],
        scratch_shapes=[
            pltpu.VMEM((virt, virt), F32),
            pltpu.VMEM((1, blocks), jnp.int32),
            pltpu.SemaphoreType.DMA,
            pltpu.SemaphoreType.DMA,
        ],
        compiler_params=pltpu.CompilerParams(vmem_limit_bytes=8 << 20),
        cost_estimate=pl.CostEstimate(
            flops=2 * virt * virt * aux_dev, bytes_accessed=2 * virt * aux_dev, transcendentals=0
        ),
        name="own_pairs",
    )(in_hbm(screen), in_hbm(own))


def cross_pairs(own, other, screen, other_screen):
    virt, aux_dev = own.shape
    blocks = other_screen.shape[1]
    half = virt // 2
    vmem = pl.BlockSpec(memory_space=VMEM)
    return pl.pallas_call(
        functools.partial(cross_pairs_kernel, blocks, aux_dev // blocks),
        in_specs=[vmem] * 4,
        out_specs=[vmem] * 2,
        out_shape=[
            jax.ShapeDtypeStruct((2 * half, half), F32),
            jax.ShapeDtypeStruct((2 * half, half), BF16),
        ],
        scratch_shapes=[pltpu.VMEM((virt, virt), F32)],
        compiler_params=pltpu.CompilerParams(vmem_limit_bytes=8 << 20),
        cost_estimate=pl.CostEstimate(
            flops=2 * virt * virt * aux_dev, bytes_accessed=4 * virt * aux_dev, transcendentals=0
        ),
        name="cross_pairs",
    )(screen, other_screen, own, other)


def symmetric(packed):
    half = packed.shape[1]
    row, col = triangle(half)
    low, both = packed[0:half, :], packed[half : 2 * half, :]
    turned = both.T
    first = jnp.where(row >= col, both, turned)
    last = jnp.where(row < col, both, turned)
    last = jnp.where(row == col, packed[2 * half : 2 * half + 1, :], last)
    top = jnp.concatenate([first, low.T], axis=1)
    return jnp.concatenate([top, jnp.concatenate([low, last], axis=1)], axis=0)


def tables_kernel(
    width, owner_ref, positions_ref, energy_ref, other_energy_ref, virt_ref,
    screen_ref, other_screen_ref, own_ref, other_ref, cross_ref, factor_ref, mask_ref,
):
    virt = own_ref.shape[0]
    virt_row = jnp.broadcast_to(virt_ref[...].astype(F32), (virt, virt))
    virt_col = virt_row.T
    energy = energy_ref[...].astype(F32)
    other_energy = other_energy_ref[...].astype(F32)
    own_row, own_col = virt_row - energy, virt_col - energy
    other_row, other_col = virt_row - other_energy, virt_col - other_energy
    own_ref[...] = 1.0 / (own_col + own_row)
    other_ref[...] = 1.0 / (other_col + other_row)
    cross_ref[...] = 1.0 / (own_col + other_row)
    blocks = owner_ref.shape[1]
    mask_ref[0:1, :] = mask_row(screen_ref[...], 0, blocks, width).astype(F32)
    mask_ref[1:2, :] = mask_row(other_screen_ref[...], 0, blocks, width).astype(F32)
    for block in range(blocks):
        where = [positions_ref[c, owner_ref[0, block]] for c in range(3)]
        rows = [
            jnp.full((1, width), where[c] * where[d], F32) for c in range(3) for d in range(3)
        ]
        factor_ref[:, block * width : (block + 1) * width] = jnp.concatenate(rows, axis=0)


def make_tables(width, owner, positions, energy, other_energy, virt_energy, screen, other_screen):
    virt, blocks = virt_energy.shape[0], owner.shape[0]
    smem = pl.BlockSpec(memory_space=SMEM)
    vmem = pl.BlockSpec(memory_space=VMEM)
    return pl.pallas_call(
        functools.partial(tables_kernel, width),
        in_specs=[smem] * 2 + [vmem] * 5,
        out_specs=[vmem] * 5,
        out_shape=[jax.ShapeDtypeStruct((virt, virt), F32)] * 3
        + [jax.ShapeDtypeStruct((rows, blocks * width), F32) for rows in (9, 2)],
        compiler_params=pltpu.CompilerParams(vmem_limit_bytes=4 << 20),
        cost_estimate=pl.CostEstimate(
            flops=16 * virt * virt, bytes_accessed=12 * virt * virt, transcendentals=0
        ),
        name="tables",
    )(
        owner.reshape(1, -1), positions,
        energy.reshape(1, 1), other_energy.reshape(1, 1), virt_energy.reshape(1, -1),
        screen, other_screen,
    )


def gamma_kernel(
    steps, own_ref, other_ref, own_inverse_ref, other_inverse_ref, cross_inverse_ref, factor_ref, mask_ref,
    own_sum_ref, other_sum_ref, cross_sum_ref, other_cross_ref,
    gamma_hbm, virial_hbm, gamma_ref, virial_ref, amps, sems, virial_sem,
):
    virt, aux_dev = own_ref.shape
    half, tile = virt // 2, aux_dev // steps
    mine = [cross_sum_ref[pl.ds(k * half, half), :] for k in range(2)]
    theirs = [other_cross_ref[pl.ds(k * half, half), :].T for k in range(2)]
    even = lax.axis_index("occ") == 0
    top = [jnp.where(even, mine[0], theirs[0]), jnp.where(even, theirs[1], mine[0])]
    bottom = [jnp.where(even, theirs[0], mine[1]), jnp.where(even, mine[1], theirs[1])]
    cross = jnp.concatenate(
        [jnp.concatenate(top, axis=1), jnp.concatenate(bottom, axis=1)], axis=0
    )
    own_amps, cross_amps, other_amps = (pl.ds(k * virt, virt) for k in range(3))
    amps[:, own_amps] = (symmetric(own_sum_ref[...]) * own_inverse_ref[...]).astype(BF16)
    amps[:, cross_amps] = (cross * cross_inverse_ref[...]).astype(BF16)
    amps[:, other_amps] = (symmetric(other_sum_ref[...]) * other_inverse_ref[...]).astype(BF16)
    copies = []
    for step in range(steps):
        columns = pl.ds(step * tile, tile)
        mask = mask_ref[:, columns].astype(BF16)
        own, other = own_ref[:, columns] * mask[0:1, :], other_ref[:, columns] * mask[1:2, :]
        cross_part = jnp.dot(amps[:, cross_amps], other, preferred_element_type=F32)
        gamma = jnp.dot(amps[:, own_amps], own, preferred_element_type=F32) + cross_part
        gamma_ref[:, columns] = gamma.astype(BF16)
        copies.append(
            pltpu.make_async_copy(
                gamma_ref.at[:, columns], gamma_hbm.at[:, columns], sems.at[step]
            )
        )
        copies[step].start()
        other_part = jnp.dot(amps[:, other_amps], other, preferred_element_type=F32)
        weight = jnp.sum(
            (gamma + cross_part) * own.astype(F32) + other_part * other.astype(F32),
            axis=0,
            keepdims=True,
        )
        virial_ref[:, columns] = factor_ref[:, columns] * weight
    copies.append(pltpu.make_async_copy(virial_ref, virial_hbm, virial_sem))
    copies[steps].start()
    for copy in copies:
        copy.wait()


def gamma_and_virial(own, other, tables, sums):
    virt, aux_dev = own.shape
    steps = 8 if aux_dev % 1024 == 0 else 1
    vmem = pl.BlockSpec(memory_space=VMEM)
    hbm = pl.BlockSpec(memory_space=pltpu.HBM)
    return pl.pallas_call(
        functools.partial(gamma_kernel, steps),
        in_specs=[vmem] * 11,
        out_specs=[hbm, hbm],
        out_shape=[
            jax.ShapeDtypeStruct((virt, aux_dev), BF16),
            jax.ShapeDtypeStruct((9, aux_dev), F32),
        ],
        scratch_shapes=[
            pltpu.VMEM((virt, aux_dev), BF16),
            pltpu.VMEM((9, aux_dev), F32),
            pltpu.VMEM((virt, 3 * virt), BF16),
            pltpu.SemaphoreType.DMA((steps,)),
            pltpu.SemaphoreType.DMA,
        ],
        compiler_params=pltpu.CompilerParams(vmem_limit_bytes=8 << 20),
        cost_estimate=pl.CostEstimate(
            flops=6 * virt * virt * aux_dev, bytes_accessed=6 * virt * aux_dev, transcendentals=0
        ),
        name="gamma_and_virial",
    )(own, other, *tables, *sums)


def swap(array, axis, size, bit):
    return lax.ppermute(array, axis, [(i, i ^ bit) for i in range(size)])


def swap_by_core(array, n_aux, bits):
    pairs = [
        (core * n_aux + i, core * n_aux + (i ^ bit))
        for core, bit in enumerate(bits)
        for i in range(n_aux)
    ]
    return lax.ppermute(array, ("occ", "aux"), pairs)


def sum_over_aux(total, send, n_aux, orders, beside=()):
    steps = list(zip(*orders))
    for step, bits in enumerate(steps):
        if step == len(steps) - 1 and beside:
            send, beside = lax.optimization_barrier((send, beside))
        total = total + swap_by_core(send, n_aux, bits).astype(F32)
        send = total.astype(BF16)
    return total, beside


def orders_of(bits):
    turned = [bits[k ^ 1] if k ^ 1 < len(bits) else bits[k] for k in range(len(bits))]
    half = len(bits) // 2
    high = bits[half:][::-1]
    return (bits, turned), (high + bits[:half], high + turned[:half])


def two_occ_body(n_aux, coeffs, occ_energy, virt_energy, screen, owner, positions):
    raw = coeffs[0]
    other = swap(raw, "occ", 2, 1)
    other_screen = swap(screen, "occ", 2, 1)
    other_energy = swap(occ_energy, "occ", 2, 1)
    cross_orders, own_orders = orders_of([1 << k for k in range(n_aux.bit_length() - 1)])
    own, own_sum, own_send = own_pairs(raw, screen)
    own_send, other_screen, other_energy = lax.optimization_barrier(
        (own_send, other_screen, other_energy)
    )
    cross_sum, cross_send = cross_pairs(own, other, screen, other_screen)
    own_sum, late = sum_over_aux(
        own_sum, own_send, n_aux, own_orders, (virt_energy, screen, other_screen, other_energy)
    )
    width = coeffs.shape[2] // screen.shape[1]
    late_virt, late_screen, late_other_screen, late_other_energy = late
    tables = make_tables(
        width, owner, positions, occ_energy, late_other_energy, late_virt, late_screen,
        late_other_screen,
    )
    own_sum, tables = lax.optimization_barrier((own_sum, tables))
    cross_sum, _ = sum_over_aux(cross_sum, cross_send, n_aux, cross_orders)
    other_sum = swap(own_sum, "occ", 2, 1)
    other_cross = swap(cross_sum, "occ", 2, 1)
    gamma, virial = gamma_and_virial(
        own, other, tables, (own_sum, other_sum, cross_sum, other_cross)
    )
    return gamma[None], virial


def general_body(n_aux, coeffs, occ_energy, virt_energy, screen, owner, positions):
    occ_dev, virt, aux_dev = coeffs.shape
    width = aux_dev // screen.shape[1]
    column_mask = jnp.repeat(screen[0], width).astype(BF16)
    masked = coeffs * column_mask[None, None, :]
    whole = lax.all_gather(masked, "occ", axis=0, tiled=True)
    energies = lax.all_gather(occ_energy, "occ", axis=0, tiled=True)
    all_rows = whole.reshape(-1, aux_dev)
    local = masked.reshape(-1, aux_dev)
    virt_f = virt_energy.astype(F32)
    spread_local = (virt_f[None, :] - occ_energy.astype(F32)[:, None]).reshape(-1)
    spread_all = (virt_f[None, :] - energies.astype(F32)[:, None]).reshape(-1)
    pairs = lax.dot_general(all_rows, local, CONTRACT_LAST, preferred_element_type=F32)
    if n_aux & (n_aux - 1):
        summed = lax.psum(pairs, "aux")
    else:
        bits = [1 << k for k in range(n_aux.bit_length() - 1)]
        summed, send = pairs, pairs.astype(BF16)
        for bit in bits:
            summed = summed + swap(send, "aux", n_aux, bit).astype(F32)
            send = summed.astype(BF16)
    amps = (summed / (spread_all[:, None] + spread_local[None, :])).astype(BF16)
    gamma = lax.dot_general(
        amps, all_rows, (((0,), (0,)), ((), ())), preferred_element_type=F32
    ).astype(BF16)
    partial_weight = jnp.sum(gamma.astype(F32) * local.astype(F32), axis=0)
    weight = lax.psum(partial_weight, "occ")
    where = jnp.repeat(positions[:, owner], width, axis=1)
    virial = (where[:, None, :] * where[None, :, :]).reshape(9, aux_dev) * weight[None, :]
    return gamma.reshape(occ_dev, virt, aux_dev), virial


def solution(mesh):
    placed = (P("occ", None, "aux"), P("occ"), P(), P("occ", "aux"), P("aux"), P())
    n_occ, n_aux = mesh.shape["occ"], mesh.shape["aux"]
    power_of_two = n_aux & (n_aux - 1) == 0

    def body(coeffs, *rest):
        fits = n_occ == 2 and coeffs.shape[0] == 1 and power_of_two
        chosen = two_occ_body if fits else general_body
        return chosen(n_aux, coeffs, *rest)

    return jax.shard_map(
        body,
        mesh=mesh,
        in_specs=placed,
        out_specs=(P("occ", None, "aux"), P(None, "aux")),
        check_vma=False,
    )
```

```python
import functools

import jax
import jax.numpy as jnp
from jax import lax
from jax.experimental import pallas as pl
from jax.experimental.pallas import tpu as pltpu
from jax.sharding import PartitionSpec as P

F32 = jnp.float32
BF16 = jnp.bfloat16
CONTRACT_LAST = (((1,), (1,)), ((), ()))
SMEM = pltpu.MemorySpace.SMEM
VMEM = pltpu.MemorySpace.VMEM
PAD = 16


def mask_row(screen, first, count, width):
    values = screen.astype(F32)
    pieces = [
        jnp.broadcast_to(values[:, k : k + 1], (1, width)) for k in range(first, first + count)
    ]
    return jnp.concatenate(pieces, axis=1).astype(BF16)


def split(aux_dev, blocks, wanted):
    steps = wanted if blocks % wanted == 0 else 1
    return steps, aux_dev // steps, blocks // steps


def triangle(size):
    return (lax.broadcasted_iota(jnp.int32, (size, size), axis) for axis in (0, 1))


def own_pairs_kernel(
    blocks, width, screen_hbm, owner_hbm, positions_hbm, own_hbm,
    own_ref, factor_ref, sum_ref, send_ref, total, screen, owner, positions, sems,
):
    half = total.shape[0] // 2
    moves = ((screen_hbm, screen), (own_hbm, own_ref), (owner_hbm, owner), (positions_hbm, positions))
    copies = [pltpu.make_async_copy(*move, sems.at[k]) for k, move in enumerate(moves)]
    for copy in copies:
        copy.start()
    copies[0].wait()
    mask = mask_row(screen[...], 0, blocks, width)
    copies[2].wait()
    copies[3].wait()
    for block in range(blocks):
        atom = owner[0, block]
        where = [positions[c, atom] for c in range(3)]
        rows = [
            jnp.full((1, width), where[c] * where[d], F32) for c in range(3) for d in range(3)
        ]
        factor_ref[:, block * width : (block + 1) * width] = jnp.concatenate(rows, axis=0)
    copies[1].wait()
    own = own_ref[...]
    total[...] = lax.dot_general(own * mask, own, CONTRACT_LAST, preferred_element_type=F32)
    low, high = pl.ds(0, half), pl.ds(half, half)
    row, col = triangle(half)
    first, last = total[low, low], total[high, high]
    diagonal = jnp.sum(jnp.where(row == col, last, 0.0), axis=0, keepdims=True)
    parts = (
        total[high, low],
        jnp.where(row >= col, first, last),
        jnp.broadcast_to(diagonal, (PAD, half)),
    )
    start = 0
    for part in parts:
        rows = pl.ds(start, part.shape[0])
        sum_ref[rows, :] = part
        send_ref[rows, :] = part.astype(BF16)
        start += part.shape[0]


def cross_pairs_kernel(
    blocks, width, screen_ref, other_screen_ref, own_ref, other_ref, sum_ref, send_ref, total
):
    half = total.shape[0] // 2
    core = lax.axis_index("occ")
    mask = mask_row(screen_ref[...] * other_screen_ref[...], 0, blocks, width)
    total[...] = lax.dot_general(
        own_ref[...], other_ref[...] * mask, CONTRACT_LAST, preferred_element_type=F32
    )
    for place in range(2):
        rows = pl.ds(place * half, half)
        straight = total[rows, pl.ds(place * half, half)]
        across = total[rows, pl.ds((1 - place) * half, half)]
        part = jnp.where(core == 0, straight, across)
        sum_ref[rows, :] = part
        send_ref[rows, :] = part.astype(BF16)


def in_hbm(array):
    return pltpu.with_memory_space_constraint(array, pltpu.HBM)


def own_pairs(own, screen, owner, positions):
    virt, aux_dev = own.shape
    blocks = screen.shape[1]
    half = virt // 2
    operands = (screen, owner.reshape(1, -1), positions, own)
    return pl.pallas_call(
        functools.partial(own_pairs_kernel, blocks, aux_dev // blocks),
        in_specs=[pl.BlockSpec(memory_space=pltpu.HBM)] * 4,
        out_specs=[pl.BlockSpec(memory_space=VMEM)] * 4,
        out_shape=[
            jax.ShapeDtypeStruct((virt, aux_dev), BF16),
            jax.ShapeDtypeStruct((9, aux_dev), F32),
            jax.ShapeDtypeStruct((2 * half + PAD, half), F32),
            jax.ShapeDtypeStruct((2 * half + PAD, half), BF16),
        ],
        scratch_shapes=[
            pltpu.VMEM((virt, virt), F32),
            pltpu.VMEM((1, blocks), jnp.int32),
            pltpu.SMEM((1, blocks), jnp.int32),
            pltpu.SMEM(positions.shape, F32),
            pltpu.SemaphoreType.DMA((4,)),
        ],
        compiler_params=pltpu.CompilerParams(vmem_limit_bytes=8 << 20),
        cost_estimate=pl.CostEstimate(
            flops=2 * virt * virt * aux_dev, bytes_accessed=2 * virt * aux_dev, transcendentals=0
        ),
        name="own_pairs",
    )(*[in_hbm(operand) for operand in operands])


def cross_pairs(own, other, screen, other_screen):
    virt, aux_dev = own.shape
    blocks = other_screen.shape[1]
    half = virt // 2
    vmem = pl.BlockSpec(memory_space=VMEM)
    return pl.pallas_call(
        functools.partial(cross_pairs_kernel, blocks, aux_dev // blocks),
        in_specs=[vmem] * 4,
        out_specs=[vmem] * 2,
        out_shape=[
            jax.ShapeDtypeStruct((2 * half, half), F32),
            jax.ShapeDtypeStruct((2 * half, half), BF16),
        ],
        scratch_shapes=[pltpu.VMEM((virt, virt), F32)],
        compiler_params=pltpu.CompilerParams(vmem_limit_bytes=8 << 20),
        cost_estimate=pl.CostEstimate(
            flops=2 * virt * virt * aux_dev, bytes_accessed=4 * virt * aux_dev, transcendentals=0
        ),
        name="cross_pairs",
    )(screen, other_screen, own, other)


def symmetric(packed):
    half = packed.shape[1]
    row, col = triangle(half)
    low, both = packed[0:half, :], packed[half : 2 * half, :]
    turned = both.T
    first = jnp.where(row >= col, both, turned)
    last = jnp.where(row < col, both, turned)
    last = jnp.where(row == col, packed[2 * half : 2 * half + 1, :], last)
    top = jnp.concatenate([first, low.T], axis=1)
    return jnp.concatenate([top, jnp.concatenate([low, last], axis=1)], axis=0)


def inverse_kernel(virt_ref, energy_ref, other_energy_ref, own_ref, cross_ref):
    half = own_ref.shape[1]
    energy, other_energy = energy_ref[...].astype(F32), other_energy_ref[...].astype(F32)
    rows = [
        jnp.broadcast_to(virt_ref[:, k * half : (k + 1) * half].astype(F32), (half, half))
        for k in range(2)
    ]
    cols = [r.T for r in rows]
    row, col = triangle(half)
    twice = [(cols[k] - energy) + (rows[k] - energy) for k in range(2)]
    own_ref[0:half, :] = 1.0 / ((cols[1] - energy) + (rows[0] - energy))
    own_ref[half : 2 * half, :] = 1.0 / jnp.where(row >= col, twice[0], twice[1])
    last = rows[1][0:PAD, :] - energy
    own_ref[2 * half : 2 * half + PAD, :] = 1.0 / (last + last)
    even = lax.axis_index("occ") == 0
    for k in range(2):
        across = jnp.where(even, rows[k], rows[1 - k]) - other_energy
        cross_ref[k * half : (k + 1) * half, :] = 1.0 / ((cols[k] - energy) + across)


def inverse_spreads(virt_energy, energy, other_energy):
    half = virt_energy.shape[0] // 2
    vmem = pl.BlockSpec(memory_space=VMEM)
    return pl.pallas_call(
        inverse_kernel,
        in_specs=[vmem] * 3,
        out_specs=[vmem] * 2,
        out_shape=[
            jax.ShapeDtypeStruct((2 * half + PAD, half), F32),
            jax.ShapeDtypeStruct((2 * half, half), F32),
        ],
        compiler_params=pltpu.CompilerParams(vmem_limit_bytes=4 << 20),
        cost_estimate=pl.CostEstimate(
            flops=32 * half * half, bytes_accessed=32 * half * half, transcendentals=0
        ),
        name="inverse_spreads",
    )(virt_energy.reshape(1, -1), energy.reshape(1, 1), other_energy.reshape(1, 1))


def own_gamma_kernel(steps, blocks, width, screen_ref, amps_ref, own_ref, part_ref, weight_ref, amps):
    tile, per_step = own_ref.shape[1] // steps, blocks // steps
    amps[...] = symmetric(amps_ref[...])
    for step in range(steps):
        columns = pl.ds(step * tile, tile)
        own = own_ref[:, columns] * mask_row(screen_ref[...], step * per_step, per_step, width)
        part = jnp.dot(amps[...], own, preferred_element_type=F32)
        part_ref[:, columns] = part
        weight_ref[:, columns] = jnp.sum(part * own.astype(F32), axis=0, keepdims=True)


def other_weight_kernel(steps, blocks, width, screen_ref, amps_ref, own_ref, first_ref, weight_ref, amps):
    tile, per_step = own_ref.shape[1] // steps, blocks // steps
    amps[...] = symmetric(amps_ref[...])
    for step in range(steps):
        columns = pl.ds(step * tile, tile)
        own = own_ref[:, columns] * mask_row(screen_ref[...], step * per_step, per_step, width)
        part = jnp.dot(amps[...], own, preferred_element_type=F32)
        weight_ref[:, columns] = first_ref[:, columns] + jnp.sum(
            part * own.astype(F32), axis=0, keepdims=True
        )


def gamma_kernel(
    steps, blocks, width, screen_ref, other_screen_ref, cross_ref, other_cross_ref, own_ref,
    other_ref, part_ref, weight_ref, factor_ref,
    gamma_hbm, virial_hbm, gamma_ref, virial_ref, amps, sems, virial_sem,
):
    virt, aux_dev = own_ref.shape
    half, tile, per_step = virt // 2, aux_dev // steps, blocks // steps
    mine = [cross_ref[pl.ds(k * half, half), :] for k in range(2)]
    theirs = [other_cross_ref[pl.ds(k * half, half), :].T for k in range(2)]
    even = lax.axis_index("occ") == 0
    low, high = pl.ds(0, half), pl.ds(half, half)
    amps[low, low] = jnp.where(even, mine[0], theirs[0])
    amps[low, high] = jnp.where(even, theirs[1], mine[0])
    amps[high, low] = jnp.where(even, theirs[0], mine[1])
    amps[high, high] = jnp.where(even, mine[1], theirs[1])
    copies = []
    for step in range(steps):
        columns = pl.ds(step * tile, tile)
        other = other_ref[:, columns]
        other = other * mask_row(other_screen_ref[...], step * per_step, per_step, width)
        cross = jnp.dot(amps[...], other, preferred_element_type=F32)
        gamma_ref[:, columns] = (part_ref[:, columns] + cross).astype(BF16)
        copies.append(
            pltpu.make_async_copy(
                gamma_ref.at[:, columns], gamma_hbm.at[:, columns], sems.at[step]
            )
        )
        copies[step].start()
        twice = jnp.sum(cross * own_ref[:, columns].astype(F32), axis=0, keepdims=True)
        mask = mask_row(screen_ref[...], step * per_step, per_step, width).astype(F32)
        weight = weight_ref[:, columns] + 2.0 * (twice * mask)
        virial_ref[:, columns] = factor_ref[:, columns] * weight
    copies.append(pltpu.make_async_copy(virial_ref, virial_hbm, virial_sem))
    copies[steps].start()
    for copy in copies:
        copy.wait()


def gamma_call(kernel, name, out_shape, screen, amps, own, *rest):
    virt, aux_dev = own.shape
    blocks = screen.shape[1]
    steps = 8 if blocks % 8 == 0 else 1
    vmem = pl.BlockSpec(memory_space=VMEM)
    return pl.pallas_call(
        functools.partial(kernel, steps, blocks, aux_dev // blocks),
        in_specs=[vmem] * (3 + len(rest)),
        out_specs=[vmem] * len(out_shape),
        out_shape=out_shape,
        scratch_shapes=[pltpu.VMEM((virt, virt), BF16)],
        compiler_params=pltpu.CompilerParams(vmem_limit_bytes=8 << 20),
        cost_estimate=pl.CostEstimate(
            flops=2 * virt * virt * aux_dev, bytes_accessed=6 * virt * aux_dev, transcendentals=0
        ),
        name=name,
    )(screen, amps, own, *rest)


def own_gamma(own, screen, amps):
    row = jax.ShapeDtypeStruct((1, own.shape[1]), F32)
    part = jax.ShapeDtypeStruct(own.shape, F32)
    return gamma_call(own_gamma_kernel, "own_gamma", [part, row], screen, amps, own)


def other_weight(other, screen, amps, weight):
    row = jax.ShapeDtypeStruct((1, other.shape[1]), F32)
    return gamma_call(other_weight_kernel, "other_weight", [row], screen, amps, other, weight)[0]


def gamma_and_virial(own, other, screen, other_screen, cross, other_cross, part, weight, factor):
    virt, aux_dev = own.shape
    blocks = screen.shape[1]
    steps = 8 if blocks % 8 == 0 else 1
    vmem = pl.BlockSpec(memory_space=VMEM)
    hbm = pl.BlockSpec(memory_space=pltpu.HBM)
    return pl.pallas_call(
        functools.partial(gamma_kernel, steps, blocks, aux_dev // blocks),
        in_specs=[vmem] * 9,
        out_specs=[hbm, hbm],
        out_shape=[
            jax.ShapeDtypeStruct((virt, aux_dev), BF16),
            jax.ShapeDtypeStruct((9, aux_dev), F32),
        ],
        scratch_shapes=[
            pltpu.VMEM((virt, aux_dev), BF16),
            pltpu.VMEM((9, aux_dev), F32),
            pltpu.VMEM((virt, virt), BF16),
            pltpu.SemaphoreType.DMA((steps,)),
            pltpu.SemaphoreType.DMA,
        ],
        compiler_params=pltpu.CompilerParams(vmem_limit_bytes=8 << 20),
        cost_estimate=pl.CostEstimate(
            flops=2 * virt * virt * aux_dev, bytes_accessed=8 * virt * aux_dev, transcendentals=0
        ),
        name="gamma_and_virial",
    )(screen, other_screen, cross, other_cross, own, other, part, weight, factor)


def swap(array, axis, size, bit):
    return lax.ppermute(array, axis, [(i, i ^ bit) for i in range(size)])


def swap_by_core(array, n_aux, bits):
    pairs = [
        (core * n_aux + i, core * n_aux + (i ^ bit))
        for core, bit in enumerate(bits)
        for i in range(n_aux)
    ]
    return lax.ppermute(array, ("occ", "aux"), pairs)


def one_round(total, send, n_aux, bits):
    total = total + swap_by_core(send, n_aux, bits).astype(F32)
    return total, total.astype(BF16)


def after(value, late):
    return lax.optimization_barrier((value, late))


def orders_of(bits):
    if len(bits) != 4:
        turned = bits[1:] + bits[:1]
        return (bits, turned), (bits, turned)
    x, y, z, w = bits
    return ([z, x, w, y], [w, y, z, x]), ([x, y, z, w], [y, x, w, z])


def two_occ_body(n_aux, coeffs, occ_energy, virt_energy, screen, owner, positions):
    raw = coeffs[0]
    other_screen = swap(screen, "occ", 2, 1)
    other_energy = swap(occ_energy, "occ", 2, 1)
    other = swap(raw, "occ", 2, 1)
    cross_orders, own_orders = orders_of([1 << k for k in range(n_aux.bit_length() - 1)])
    own, factor, own_sum, own_send = own_pairs(raw, screen, owner, positions)
    cross_sum, cross_send = cross_pairs(own, other, screen, other_screen)
    rounds = len(own_orders[0])
    energy = occ_energy
    for step in range(rounds):
        if step == rounds - 2:
            own_send, other_energy = after(own_send, other_energy)
            energy = swap(other_energy, "occ", 2, 1)
        if step == rounds - 1:
            own_send, late = after(own_send, (virt_energy, energy, other_energy))
            virt_energy, energy, other_energy = late
        own_sum, own_send = one_round(own_sum, own_send, n_aux, [o[step] for o in own_orders])
    own_inverse, cross_inverse = inverse_spreads(virt_energy, energy, other_energy)
    own_amps = (own_sum * own_inverse).astype(BF16)
    part, weight = own_gamma(own, screen, own_amps)
    for step in range(rounds):
        cross_sum, cross_send = one_round(
            cross_sum, cross_send, n_aux, [o[step] for o in cross_orders]
        )
    cross = (cross_sum * cross_inverse).astype(BF16)
    own_amps, part = after(own_amps, part)
    other_amps = swap(own_amps, "occ", 2, 1)
    other_cross = swap(cross, "occ", 2, 1)
    weight = other_weight(other, other_screen, other_amps, weight)
    gamma, virial = gamma_and_virial(
        own, other, screen, other_screen, cross, other_cross, part, weight, factor
    )
    return gamma[None], virial


def general_body(n_aux, coeffs, occ_energy, virt_energy, screen, owner, positions):
    occ_dev, virt, aux_dev = coeffs.shape
    width = aux_dev // screen.shape[1]
    column_mask = jnp.repeat(screen[0], width).astype(BF16)
    masked = coeffs * column_mask[None, None, :]
    whole = lax.all_gather(masked, "occ", axis=0, tiled=True)
    energies = lax.all_gather(occ_energy, "occ", axis=0, tiled=True)
    all_rows = whole.reshape(-1, aux_dev)
    local = masked.reshape(-1, aux_dev)
    virt_f = virt_energy.astype(F32)
    spread_local = (virt_f[None, :] - occ_energy.astype(F32)[:, None]).reshape(-1)
    spread_all = (virt_f[None, :] - energies.astype(F32)[:, None]).reshape(-1)
    pairs = lax.dot_general(all_rows, local, CONTRACT_LAST, preferred_element_type=F32)
    if n_aux & (n_aux - 1):
        summed = lax.psum(pairs, "aux")
    else:
        bits = [1 << k for k in range(n_aux.bit_length() - 1)]
        summed, send = pairs, pairs.astype(BF16)
        for bit in bits:
            summed = summed + swap(send, "aux", n_aux, bit).astype(F32)
            send = summed.astype(BF16)
    amps = (summed / (spread_all[:, None] + spread_local[None, :])).astype(BF16)
    gamma = lax.dot_general(
        amps, all_rows, (((0,), (0,)), ((), ())), preferred_element_type=F32
    ).astype(BF16)
    partial_weight = jnp.sum(gamma.astype(F32) * local.astype(F32), axis=0)
    weight = lax.psum(partial_weight, "occ")
    where = jnp.repeat(positions[:, owner], width, axis=1)
    virial = (where[:, None, :] * where[None, :, :]).reshape(9, aux_dev) * weight[None, :]
    return gamma.reshape(occ_dev, virt, aux_dev), virial


def solution(mesh):
    placed = (P("occ", None, "aux"), P("occ"), P(), P("occ", "aux"), P("aux"), P())
    n_occ, n_aux = mesh.shape["occ"], mesh.shape["aux"]
    power_of_two = n_aux & (n_aux - 1) == 0

    def body(coeffs, *rest):
        fits = n_occ == 2 and coeffs.shape[0] == 1 and power_of_two
        chosen = two_occ_body if fits else general_body
        return chosen(n_aux, coeffs, *rest)

    return jax.shard_map(
        body,
        mesh=mesh,
        in_specs=placed,
        out_specs=(P("occ", None, "aux"), P(None, "aux")),
        check_vma=False,
    )
```

```python
import functools

import jax
import jax.numpy as jnp
from jax import lax
from jax.experimental import pallas as pl
from jax.experimental.pallas import tpu as pltpu
from jax.sharding import PartitionSpec as P

F32 = jnp.float32
BF16 = jnp.bfloat16
CONTRACT_LAST = (((1,), (1,)), ((), ()))
SMEM = pltpu.MemorySpace.SMEM
VMEM = pltpu.MemorySpace.VMEM
LANES = 128
PAD = 16


def mask_row(screen, first, count, width):
    values = screen.astype(F32)
    pieces = [
        jnp.broadcast_to(values[:, k : k + 1], (1, width)) for k in range(first, first + count)
    ]
    return jnp.concatenate(pieces, axis=1).astype(BF16)


def split(aux_dev, blocks, wanted):
    steps = wanted if blocks % wanted == 0 else 1
    return steps, aux_dev // steps, blocks // steps


def triangle(size):
    return (lax.broadcasted_iota(jnp.int32, (size, size), axis) for axis in (0, 1))


def own_pairs_kernel(
    blocks, width, screen_hbm, owner_hbm, positions_hbm, own_hbm,
    own_ref, factor_ref, sum_ref, send_ref, total, screen, owner, positions, sems,
):
    half = total.shape[0] // 2
    moves = ((screen_hbm, screen), (own_hbm, own_ref), (owner_hbm, owner), (positions_hbm, positions))
    copies = [pltpu.make_async_copy(*move, sems.at[k]) for k, move in enumerate(moves)]
    for copy in copies:
        copy.start()
    copies[0].wait()
    mask = mask_row(screen[...], 0, blocks, width)
    copies[2].wait()
    copies[3].wait()
    for block in range(blocks):
        atom = owner[0, block]
        where = [positions[c, atom] for c in range(3)]
        rows = [
            jnp.full((1, width), where[c] * where[d], F32) for c in range(3) for d in range(3)
        ]
        factor_ref[:, block * width : (block + 1) * width] = jnp.concatenate(rows, axis=0)
    copies[1].wait()
    own = own_ref[...]
    total[...] = lax.dot_general(own * mask, own, CONTRACT_LAST, preferred_element_type=F32)
    low, high = pl.ds(0, half), pl.ds(half, half)
    row, col = triangle(half)
    first, last = total[low, low], total[high, high]
    diagonal = jnp.sum(jnp.where(row == col, last, 0.0), axis=0, keepdims=True)
    parts = (
        total[high, low],
        jnp.where(row >= col, first, last),
        jnp.broadcast_to(diagonal, (PAD, half)),
    )
    start = 0
    for part in parts:
        rows = pl.ds(start, part.shape[0])
        sum_ref[rows, :] = part
        send_ref[rows, :] = part.astype(BF16)
        start += part.shape[0]


def cross_pairs_kernel(
    blocks, width, screen_ref, other_screen_ref, own_ref, other_ref, sum_ref, send_ref, total
):
    half = total.shape[0] // 2
    core = lax.axis_index("occ")
    mask = mask_row(screen_ref[...] * other_screen_ref[...], 0, blocks, width)
    total[...] = lax.dot_general(
        own_ref[...], other_ref[...] * mask, CONTRACT_LAST, preferred_element_type=F32
    )
    for place in range(2):
        rows = pl.ds(place * half, half)
        straight = total[rows, pl.ds(place * half, half)]
        across = total[rows, pl.ds((1 - place) * half, half)]
        part = jnp.where(core == 0, straight, across)
        sum_ref[rows, :] = part
        send_ref[rows, :] = part.astype(BF16)


def in_hbm(array):
    return pltpu.with_memory_space_constraint(array, pltpu.HBM)


def own_pairs(own, screen, owner, positions):
    virt, aux_dev = own.shape
    blocks = screen.shape[1]
    half = virt // 2
    operands = (screen, owner.reshape(1, -1), positions, own)
    return pl.pallas_call(
        functools.partial(own_pairs_kernel, blocks, aux_dev // blocks),
        in_specs=[pl.BlockSpec(memory_space=pltpu.HBM)] * 4,
        out_specs=[pl.BlockSpec(memory_space=VMEM)] * 4,
        out_shape=[
            jax.ShapeDtypeStruct((virt, aux_dev), BF16),
            jax.ShapeDtypeStruct((9, aux_dev), F32),
            jax.ShapeDtypeStruct((2 * half + PAD, half), F32),
            jax.ShapeDtypeStruct((2 * half + PAD, half), BF16),
        ],
        scratch_shapes=[
            pltpu.VMEM((virt, virt), F32),
            pltpu.VMEM((1, blocks), jnp.int32),
            pltpu.SMEM((1, blocks), jnp.int32),
            pltpu.SMEM(positions.shape, F32),
            pltpu.SemaphoreType.DMA((4,)),
        ],
        compiler_params=pltpu.CompilerParams(vmem_limit_bytes=8 << 20),
        cost_estimate=pl.CostEstimate(
            flops=2 * virt * virt * aux_dev, bytes_accessed=2 * virt * aux_dev, transcendentals=0
        ),
        name="own_pairs",
    )(*[in_hbm(operand) for operand in operands])


def cross_pairs(own, other, screen, other_screen):
    virt, aux_dev = own.shape
    blocks = other_screen.shape[1]
    half = virt // 2
    vmem = pl.BlockSpec(memory_space=VMEM)
    return pl.pallas_call(
        functools.partial(cross_pairs_kernel, blocks, aux_dev // blocks),
        in_specs=[vmem] * 4,
        out_specs=[vmem] * 2,
        out_shape=[
            jax.ShapeDtypeStruct((2 * half, half), F32),
            jax.ShapeDtypeStruct((2 * half, half), BF16),
        ],
        scratch_shapes=[pltpu.VMEM((virt, virt), F32)],
        compiler_params=pltpu.CompilerParams(vmem_limit_bytes=8 << 20),
        cost_estimate=pl.CostEstimate(
            flops=8 * virt * virt * aux_dev, bytes_accessed=16 * virt * aux_dev, transcendentals=0
        ),
        name="cross_pairs",
    )(screen, other_screen, own, other)


def symmetric(packed):
    half = packed.shape[1]
    row, col = triangle(half)
    low, both = packed[0:half, :], packed[half : 2 * half, :]
    turned = both.T
    first = jnp.where(row >= col, both, turned)
    last = jnp.where(row < col, both, turned)
    last = jnp.where(row == col, packed[2 * half : 2 * half + 1, :], last)
    top = jnp.concatenate([first, low.T], axis=1)
    return jnp.concatenate([top, jnp.concatenate([low, last], axis=1)], axis=0)


def inverse_kernel(virt_ref, energy_ref, other_energy_ref, own_ref, cross_ref):
    half = own_ref.shape[1]
    energy, other_energy = (
        ref[...].astype(F32)[0:1, 0:1] for ref in (energy_ref, other_energy_ref)
    )
    rows = [
        jnp.broadcast_to(virt_ref[:, k * half : (k + 1) * half].astype(F32), (half, half))
        for k in range(2)
    ]
    cols = [r.T for r in rows]
    row, col = triangle(half)
    twice = [(cols[k] - energy) + (rows[k] - energy) for k in range(2)]
    own_ref[0:half, :] = 1.0 / ((cols[1] - energy) + (rows[0] - energy))
    own_ref[half : 2 * half, :] = 1.0 / jnp.where(row >= col, twice[0], twice[1])
    last = rows[1][0:PAD, :] - energy
    own_ref[2 * half : 2 * half + PAD, :] = 1.0 / (last + last)
    even = lax.axis_index("occ") == 0
    for k in range(2):
        across = jnp.where(even, rows[k], rows[1 - k]) - other_energy
        cross_ref[k * half : (k + 1) * half, :] = 1.0 / ((cols[k] - energy) + across)


def inverse_spreads(virt_energy, energy, other_energy):
    half = virt_energy.shape[0] // 2
    vmem = pl.BlockSpec(memory_space=VMEM)
    return pl.pallas_call(
        inverse_kernel,
        in_specs=[vmem] * 3,
        out_specs=[vmem] * 2,
        out_shape=[
            jax.ShapeDtypeStruct((2 * half + PAD, half), F32),
            jax.ShapeDtypeStruct((2 * half, half), F32),
        ],
        compiler_params=pltpu.CompilerParams(vmem_limit_bytes=4 << 20),
        cost_estimate=pl.CostEstimate(
            flops=32 * half * half, bytes_accessed=32 * half * half, transcendentals=0
        ),
        name="inverse_spreads",
    )(virt_energy.reshape(1, -1), energy.reshape(1, -1), other_energy.reshape(1, -1))


def own_gamma_kernel(
    steps, blocks, width, screen_ref, amps_ref, own_ref, masked_ref, part_ref, weight_ref, amps
):
    tile, per_step = own_ref.shape[1] // steps, blocks // steps
    amps[...] = symmetric(amps_ref[...])
    for step in range(steps):
        columns = pl.ds(step * tile, tile)
        own = own_ref[:, columns] * mask_row(screen_ref[...], step * per_step, per_step, width)
        part = jnp.dot(amps[...], own, preferred_element_type=F32)
        masked_ref[:, columns] = own
        part_ref[:, columns] = part
        weight_ref[:, columns] = jnp.sum(part * own.astype(F32), axis=0, keepdims=True)


def other_weight_kernel(
    steps, blocks, width, screen_ref, amps_ref, own_ref, first_ref, masked_ref, weight_ref, amps
):
    tile, per_step = own_ref.shape[1] // steps, blocks // steps
    amps[...] = symmetric(amps_ref[...])
    for step in range(steps):
        columns = pl.ds(step * tile, tile)
        own = own_ref[:, columns] * mask_row(screen_ref[...], step * per_step, per_step, width)
        part = jnp.dot(amps[...], own, preferred_element_type=F32)
        masked_ref[:, columns] = own
        weight_ref[:, columns] = first_ref[:, columns] + jnp.sum(
            part * own.astype(F32), axis=0, keepdims=True
        )


def gamma_kernel(
    steps, cross_ref, other_cross_ref, own_ref, other_ref, part_ref, weight_ref, factor_ref,
    gamma_hbm, virial_hbm, gamma_ref, virial_ref, amps, sems, virial_sem,
):
    virt, aux_dev = own_ref.shape
    half, tile = virt // 2, aux_dev // steps
    mine = [cross_ref[pl.ds(k * half, half), :] for k in range(2)]
    theirs = [other_cross_ref[pl.ds(k * half, half), :].T for k in range(2)]
    even = lax.axis_index("occ") == 0
    low, high = pl.ds(0, half), pl.ds(half, half)
    amps[low, low] = jnp.where(even, mine[0], theirs[0])
    amps[low, high] = jnp.where(even, theirs[1], mine[0])
    amps[high, low] = jnp.where(even, theirs[0], mine[1])
    amps[high, high] = jnp.where(even, mine[1], theirs[1])
    copies = []
    for step in range(steps):
        columns = pl.ds(step * tile, tile)
        cross = jnp.dot(amps[...], other_ref[:, columns], preferred_element_type=F32)
        gamma_ref[:, columns] = (part_ref[:, columns] + cross).astype(BF16)
        copies.append(
            pltpu.make_async_copy(
                gamma_ref.at[:, columns], gamma_hbm.at[:, columns], sems.at[step]
            )
        )
        copies[step].start()
        twice = jnp.sum(cross * own_ref[:, columns].astype(F32), axis=0, keepdims=True)
        virial_ref[:, columns] = factor_ref[:, columns] * (weight_ref[:, columns] + 2.0 * twice)
    copies.append(pltpu.make_async_copy(virial_ref, virial_hbm, virial_sem))
    copies[steps].start()
    for copy in copies:
        copy.wait()


def gamma_call(kernel, name, out_shape, screen, amps, own, *rest):
    virt, aux_dev = own.shape
    blocks = screen.shape[1]
    steps = 8 if blocks % 8 == 0 else 1
    vmem = pl.BlockSpec(memory_space=VMEM)
    return pl.pallas_call(
        functools.partial(kernel, steps, blocks, aux_dev // blocks),
        in_specs=[vmem] * (3 + len(rest)),
        out_specs=[vmem] * len(out_shape),
        out_shape=out_shape,
        scratch_shapes=[pltpu.VMEM((virt, virt), BF16)],
        compiler_params=pltpu.CompilerParams(vmem_limit_bytes=8 << 20),
        cost_estimate=pl.CostEstimate(
            flops=2 * virt * virt * aux_dev, bytes_accessed=6 * virt * aux_dev, transcendentals=0
        ),
        name=name,
    )(screen, amps, own, *rest)


def own_gamma(own, screen, amps):
    row = jax.ShapeDtypeStruct((1, own.shape[1]), F32)
    part = jax.ShapeDtypeStruct(own.shape, F32)
    masked = jax.ShapeDtypeStruct(own.shape, BF16)
    return gamma_call(own_gamma_kernel, "own_gamma", [masked, part, row], screen, amps, own)


def other_weight(other, screen, amps, weight):
    row = jax.ShapeDtypeStruct((1, other.shape[1]), F32)
    masked = jax.ShapeDtypeStruct(other.shape, BF16)
    return gamma_call(
        other_weight_kernel, "other_weight", [masked, row], screen, amps, other, weight
    )


def gamma_and_virial(own, other, cross, other_cross, part, weight, factor):
    virt, aux_dev = own.shape
    steps = 8 if aux_dev % 1024 == 0 else 1
    vmem = pl.BlockSpec(memory_space=VMEM)
    hbm = pl.BlockSpec(memory_space=pltpu.HBM)
    return pl.pallas_call(
        functools.partial(gamma_kernel, steps),
        in_specs=[vmem] * 7,
        out_specs=[hbm, hbm],
        out_shape=[
            jax.ShapeDtypeStruct((virt, aux_dev), BF16),
            jax.ShapeDtypeStruct((9, aux_dev), F32),
        ],
        scratch_shapes=[
            pltpu.VMEM((virt, aux_dev), BF16),
            pltpu.VMEM((9, aux_dev), F32),
            pltpu.VMEM((virt, virt), BF16),
            pltpu.SemaphoreType.DMA((steps,)),
            pltpu.SemaphoreType.DMA,
        ],
        compiler_params=pltpu.CompilerParams(vmem_limit_bytes=8 << 20),
        cost_estimate=pl.CostEstimate(
            flops=2 * virt * virt * aux_dev, bytes_accessed=8 * virt * aux_dev, transcendentals=0
        ),
        name="gamma_and_virial",
    )(cross, other_cross, own, other, part, weight, factor)


def swap(array, axis, size, bit):
    return lax.ppermute(array, axis, [(i, i ^ bit) for i in range(size)])


def swap_by_core(array, n_aux, bits):
    pairs = [
        (core * n_aux + i, core * n_aux + (i ^ bit))
        for core, bit in enumerate(bits)
        for i in range(n_aux)
    ]
    return lax.ppermute(array, ("occ", "aux"), pairs)


def one_round(total, send, n_aux, bits):
    total = total + swap_by_core(send, n_aux, bits).astype(F32)
    return total, total.astype(BF16)


def after(value, late):
    return lax.optimization_barrier((value, late))


def orders_of(bits):
    if len(bits) != 4:
        turned = bits[1:] + bits[:1]
        return (bits, turned), (bits, turned)
    x, y, z, w = bits
    return ([x, y, z, w], [y, x, w, z]), ([x, w, z, y], [y, z, w, x])


def two_occ_body(n_aux, coeffs, occ_energy, virt_energy, screen, owner, positions):
    raw = coeffs[0]
    other_screen = swap(screen, "occ", 2, 1)
    other = swap(raw, "occ", 2, 1)
    cross_orders, own_orders = orders_of([1 << k for k in range(n_aux.bit_length() - 1)])
    own, factor, own_sum, own_send = own_pairs(raw, screen, owner, positions)
    cross_sum, cross_send = cross_pairs(own, other, screen, other_screen)
    rounds = len(own_orders[0])
    energy = jnp.pad(occ_energy, (0, LANES - 1))
    cross_send, energy = after(cross_send, energy)
    other_energy = swap(energy, "occ", 2, 1)
    inverses = inverse_spreads(virt_energy, energy, other_energy)
    first_cross = cross_send
    for step in range(rounds):
        if step == 1:
            own_send, _ = after(own_send, first_cross)
        if step == rounds // 2:
            cross_send, inverses = after(cross_send, inverses)
        own_sum, own_send = one_round(own_sum, own_send, n_aux, [o[step] for o in own_orders])
        cross_sum, cross_send = one_round(
            cross_sum, cross_send, n_aux, [o[step] for o in cross_orders]
        )
    own_inverse, cross_inverse = inverses
    own_amps = (own_sum * own_inverse).astype(BF16)
    own, part, weight = own_gamma(own, screen, own_amps)
    cross = (cross_sum * cross_inverse).astype(BF16)
    cross, part = after(cross, part)
    other_amps = swap(own_amps, "occ", 2, 1)
    other_cross = swap(cross, "occ", 2, 1)
    other, weight = other_weight(other, other_screen, other_amps, weight)
    gamma, virial = gamma_and_virial(own, other, cross, other_cross, part, weight, factor)
    return gamma[None], virial


def general_body(n_aux, coeffs, occ_energy, virt_energy, screen, owner, positions):
    occ_dev, virt, aux_dev = coeffs.shape
    width = aux_dev // screen.shape[1]
    column_mask = jnp.repeat(screen[0], width).astype(BF16)
    masked = coeffs * column_mask[None, None, :]
    whole = lax.all_gather(masked, "occ", axis=0, tiled=True)
    energies = lax.all_gather(occ_energy, "occ", axis=0, tiled=True)
    all_rows = whole.reshape(-1, aux_dev)
    local = masked.reshape(-1, aux_dev)
    virt_f = virt_energy.astype(F32)
    spread_local = (virt_f[None, :] - occ_energy.astype(F32)[:, None]).reshape(-1)
    spread_all = (virt_f[None, :] - energies.astype(F32)[:, None]).reshape(-1)
    pairs = lax.dot_general(all_rows, local, CONTRACT_LAST, preferred_element_type=F32)
    if n_aux & (n_aux - 1):
        summed = lax.psum(pairs, "aux")
    else:
        bits = [1 << k for k in range(n_aux.bit_length() - 1)]
        summed, send = pairs, pairs.astype(BF16)
        for bit in bits:
            summed = summed + swap(send, "aux", n_aux, bit).astype(F32)
            send = summed.astype(BF16)
    amps = (summed / (spread_all[:, None] + spread_local[None, :])).astype(BF16)
    gamma = lax.dot_general(
        amps, all_rows, (((0,), (0,)), ((), ())), preferred_element_type=F32
    ).astype(BF16)
    partial_weight = jnp.sum(gamma.astype(F32) * local.astype(F32), axis=0)
    weight = lax.psum(partial_weight, "occ")
    where = jnp.repeat(positions[:, owner], width, axis=1)
    virial = (where[:, None, :] * where[None, :, :]).reshape(9, aux_dev) * weight[None, :]
    return gamma.reshape(occ_dev, virt, aux_dev), virial


def solution(mesh):
    placed = (P("occ", None, "aux"), P("occ"), P(), P("occ", "aux"), P("aux"), P())
    n_occ, n_aux = mesh.shape["occ"], mesh.shape["aux"]
    power_of_two = n_aux & (n_aux - 1) == 0

    def body(coeffs, *rest):
        even_halves = coeffs.shape[1] % (2 * LANES) == 0
        fits = n_occ == 2 and coeffs.shape[0] == 1 and power_of_two and even_halves
        chosen = two_occ_body if fits else general_body
        return chosen(n_aux, coeffs, *rest)

    return jax.shard_map(
        body,
        mesh=mesh,
        in_specs=placed,
        out_specs=(P("occ", None, "aux"), P(None, "aux")),
        check_vma=False,
    )
```

```python
import functools

import jax
import jax.numpy as jnp
from jax import lax
from jax.experimental import pallas as pl
from jax.experimental.pallas import tpu as pltpu
from jax.sharding import PartitionSpec as P

F32 = jnp.float32
BF16 = jnp.bfloat16
CONTRACT_LAST = (((1,), (1,)), ((), ()))
SMEM = pltpu.MemorySpace.SMEM
VMEM = pltpu.MemorySpace.VMEM
LANES = 128
PAD = 16


def mask_row(screen, first, count, width):
    values = screen.astype(F32)
    pieces = [
        jnp.broadcast_to(values[:, k : k + 1], (1, width)) for k in range(first, first + count)
    ]
    return jnp.concatenate(pieces, axis=1).astype(BF16)


def split(aux_dev, blocks, wanted):
    steps = wanted if blocks % wanted == 0 else 1
    return steps, aux_dev // steps, blocks // steps


def triangle(size):
    return (lax.broadcasted_iota(jnp.int32, (size, size), axis) for axis in (0, 1))


def own_pairs_kernel(
    blocks, width, screen_hbm, owner_hbm, positions_hbm, own_hbm,
    own_ref, factor_ref, sum_ref, send_ref, total, screen, owner, positions, sems,
):
    half = total.shape[0] // 2
    moves = ((screen_hbm, screen), (own_hbm, own_ref), (owner_hbm, owner), (positions_hbm, positions))
    copies = [pltpu.make_async_copy(*move, sems.at[k]) for k, move in enumerate(moves)]
    for copy in copies:
        copy.start()
    copies[0].wait()
    mask = mask_row(screen[...], 0, blocks, width)
    copies[2].wait()
    copies[3].wait()
    for block in range(blocks):
        atom = owner[0, block]
        where = [positions[c, atom] for c in range(3)]
        rows = [
            jnp.full((1, width), where[c] * where[d], F32) for c in range(3) for d in range(3)
        ]
        factor_ref[:, block * width : (block + 1) * width] = jnp.concatenate(rows, axis=0)
    copies[1].wait()
    own = own_ref[...]
    total[...] = lax.dot_general(own * mask, own, CONTRACT_LAST, preferred_element_type=F32)
    low, high = pl.ds(0, half), pl.ds(half, half)
    row, col = triangle(half)
    first, last = total[low, low], total[high, high]
    diagonal = jnp.sum(jnp.where(row == col, last, 0.0), axis=0, keepdims=True)
    parts = (
        total[high, low],
        jnp.where(row >= col, first, last),
        jnp.broadcast_to(diagonal, (PAD, half)),
    )
    start = 0
    for part in parts:
        rows = pl.ds(start, part.shape[0])
        sum_ref[rows, :] = part
        send_ref[rows, :] = part.astype(BF16)
        start += part.shape[0]


def cross_pairs_kernel(
    blocks, width, screen_ref, other_screen_ref, own_ref, other_ref, sum_ref, send_ref, total
):
    half = total.shape[0] // 2
    core = lax.axis_index("occ")
    mask = mask_row(screen_ref[...] * other_screen_ref[...], 0, blocks, width)
    total[...] = lax.dot_general(
        own_ref[...], other_ref[...] * mask, CONTRACT_LAST, preferred_element_type=F32
    )
    for place in range(2):
        rows = pl.ds(place * half, half)
        straight = total[rows, pl.ds(place * half, half)]
        across = total[rows, pl.ds((1 - place) * half, half)]
        part = jnp.where(core == 0, straight, across)
        sum_ref[rows, :] = part
        send_ref[rows, :] = part.astype(BF16)


def in_hbm(array):
    return pltpu.with_memory_space_constraint(array, pltpu.HBM)


def own_pairs(own, screen, owner, positions):
    virt, aux_dev = own.shape
    blocks = screen.shape[1]
    half = virt // 2
    operands = (screen, owner.reshape(1, -1), positions, own)
    return pl.pallas_call(
        functools.partial(own_pairs_kernel, blocks, aux_dev // blocks),
        in_specs=[pl.BlockSpec(memory_space=pltpu.HBM)] * 4,
        out_specs=[pl.BlockSpec(memory_space=VMEM)] * 4,
        out_shape=[
            jax.ShapeDtypeStruct((virt, aux_dev), BF16),
            jax.ShapeDtypeStruct((9, aux_dev), F32),
            jax.ShapeDtypeStruct((2 * half + PAD, half), F32),
            jax.ShapeDtypeStruct((2 * half + PAD, half), BF16),
        ],
        scratch_shapes=[
            pltpu.VMEM((virt, virt), F32),
            pltpu.VMEM((1, blocks), jnp.int32),
            pltpu.SMEM((1, blocks), jnp.int32),
            pltpu.SMEM(positions.shape, F32),
            pltpu.SemaphoreType.DMA((4,)),
        ],
        compiler_params=pltpu.CompilerParams(vmem_limit_bytes=8 << 20),
        cost_estimate=pl.CostEstimate(
            flops=2 * virt * virt * aux_dev, bytes_accessed=2 * virt * aux_dev, transcendentals=0
        ),
        name="own_pairs",
    )(*[in_hbm(operand) for operand in operands])


def cross_pairs(own, other, screen, other_screen):
    virt, aux_dev = own.shape
    blocks = other_screen.shape[1]
    half = virt // 2
    vmem = pl.BlockSpec(memory_space=VMEM)
    return pl.pallas_call(
        functools.partial(cross_pairs_kernel, blocks, aux_dev // blocks),
        in_specs=[vmem] * 4,
        out_specs=[vmem] * 2,
        out_shape=[
            jax.ShapeDtypeStruct((2 * half, half), F32),
            jax.ShapeDtypeStruct((2 * half, half), BF16),
        ],
        scratch_shapes=[pltpu.VMEM((virt, virt), F32)],
        compiler_params=pltpu.CompilerParams(vmem_limit_bytes=8 << 20),
        cost_estimate=pl.CostEstimate(
            flops=8 * virt * virt * aux_dev, bytes_accessed=16 * virt * aux_dev, transcendentals=0
        ),
        name="cross_pairs",
    )(screen, other_screen, own, other)


def symmetric(packed):
    half = packed.shape[1]
    row, col = triangle(half)
    low, both = packed[0:half, :], packed[half : 2 * half, :]
    turned = both.T
    first = jnp.where(row >= col, both, turned)
    last = jnp.where(row < col, both, turned)
    last = jnp.where(row == col, packed[2 * half : 2 * half + 1, :], last)
    top = jnp.concatenate([first, low.T], axis=1)
    return jnp.concatenate([top, jnp.concatenate([low, last], axis=1)], axis=0)


def inverse_kernel(virt_ref, energy_ref, other_energy_ref, own_ref, cross_ref):
    half = own_ref.shape[1]
    energy, other_energy = (
        ref[...].astype(F32)[0:1, 0:1] for ref in (energy_ref, other_energy_ref)
    )
    rows = [
        jnp.broadcast_to(virt_ref[:, k * half : (k + 1) * half].astype(F32), (half, half))
        for k in range(2)
    ]
    cols = [r.T for r in rows]
    row, col = triangle(half)
    twice = [(cols[k] - energy) + (rows[k] - energy) for k in range(2)]
    own_ref[0:half, :] = 1.0 / ((cols[1] - energy) + (rows[0] - energy))
    own_ref[half : 2 * half, :] = 1.0 / jnp.where(row >= col, twice[0], twice[1])
    last = rows[1][0:PAD, :] - energy
    own_ref[2 * half : 2 * half + PAD, :] = 1.0 / (last + last)
    even = lax.axis_index("occ") == 0
    for k in range(2):
        across = jnp.where(even, rows[k], rows[1 - k]) - other_energy
        cross_ref[k * half : (k + 1) * half, :] = 1.0 / ((cols[k] - energy) + across)


def inverse_spreads(virt_energy, energy, other_energy):
    half = virt_energy.shape[0] // 2
    vmem = pl.BlockSpec(memory_space=VMEM)
    return pl.pallas_call(
        inverse_kernel,
        in_specs=[vmem] * 3,
        out_specs=[vmem] * 2,
        out_shape=[
            jax.ShapeDtypeStruct((2 * half + PAD, half), F32),
            jax.ShapeDtypeStruct((2 * half, half), F32),
        ],
        compiler_params=pltpu.CompilerParams(vmem_limit_bytes=4 << 20),
        cost_estimate=pl.CostEstimate(
            flops=32 * half * half, bytes_accessed=32 * half * half, transcendentals=0
        ),
        name="inverse_spreads",
    )(virt_energy.reshape(1, -1), energy.reshape(1, -1), other_energy.reshape(1, -1))


def own_gamma_kernel(
    steps, blocks, width, screen_ref, amps_ref, own_ref, masked_ref, part_ref, weight_ref, amps
):
    tile, per_step = own_ref.shape[1] // steps, blocks // steps
    amps[...] = symmetric(amps_ref[...])
    for step in range(steps):
        columns = pl.ds(step * tile, tile)
        own = own_ref[:, columns] * mask_row(screen_ref[...], step * per_step, per_step, width)
        part = jnp.dot(amps[...], own, preferred_element_type=F32)
        masked_ref[:, columns] = own
        part_ref[:, columns] = part
        weight_ref[:, columns] = jnp.sum(part * own.astype(F32), axis=0, keepdims=True)


def other_weight_kernel(
    steps, blocks, width, screen_ref, amps_ref, own_ref, first_ref, masked_ref, weight_ref, amps
):
    tile, per_step = own_ref.shape[1] // steps, blocks // steps
    amps[...] = symmetric(amps_ref[...])
    for step in range(steps):
        columns = pl.ds(step * tile, tile)
        own = own_ref[:, columns] * mask_row(screen_ref[...], step * per_step, per_step, width)
        part = jnp.dot(amps[...], own, preferred_element_type=F32)
        masked_ref[:, columns] = own
        weight_ref[:, columns] = first_ref[:, columns] + jnp.sum(
            part * own.astype(F32), axis=0, keepdims=True
        )


def gamma_kernel(
    steps, cross_ref, other_cross_ref, own_ref, other_ref, part_ref, weight_ref, factor_ref,
    gamma_hbm, virial_hbm, gamma_ref, virial_ref, amps, sems, virial_sem,
):
    virt, aux_dev = own_ref.shape
    half, tile = virt // 2, aux_dev // steps
    mine = [cross_ref[pl.ds(k * half, half), :] for k in range(2)]
    theirs = [other_cross_ref[pl.ds(k * half, half), :].T for k in range(2)]
    even = lax.axis_index("occ") == 0
    low, high = pl.ds(0, half), pl.ds(half, half)
    amps[low, low] = jnp.where(even, mine[0], theirs[0])
    amps[low, high] = jnp.where(even, theirs[1], mine[0])
    amps[high, low] = jnp.where(even, theirs[0], mine[1])
    amps[high, high] = jnp.where(even, mine[1], theirs[1])
    copies = []
    for step in range(steps):
        columns = pl.ds(step * tile, tile)
        cross = jnp.dot(amps[...], other_ref[:, columns], preferred_element_type=F32)
        gamma_ref[:, columns] = (part_ref[:, columns] + cross).astype(BF16)
        copies.append(
            pltpu.make_async_copy(
                gamma_ref.at[:, columns], gamma_hbm.at[:, columns], sems.at[step]
            )
        )
        copies[step].start()
        twice = jnp.sum(cross * own_ref[:, columns].astype(F32), axis=0, keepdims=True)
        virial_ref[:, columns] = factor_ref[:, columns] * (weight_ref[:, columns] + 2.0 * twice)
    copies.append(pltpu.make_async_copy(virial_ref, virial_hbm, virial_sem))
    copies[steps].start()
    for copy in copies:
        copy.wait()


def gamma_call(kernel, name, out_shape, screen, amps, own, *rest):
    virt, aux_dev = own.shape
    blocks = screen.shape[1]
    steps = 8 if blocks % 8 == 0 else 1
    vmem = pl.BlockSpec(memory_space=VMEM)
    return pl.pallas_call(
        functools.partial(kernel, steps, blocks, aux_dev // blocks),
        in_specs=[vmem] * (3 + len(rest)),
        out_specs=[vmem] * len(out_shape),
        out_shape=out_shape,
        scratch_shapes=[pltpu.VMEM((virt, virt), BF16)],
        compiler_params=pltpu.CompilerParams(vmem_limit_bytes=8 << 20),
        cost_estimate=pl.CostEstimate(
            flops=2 * virt * virt * aux_dev, bytes_accessed=6 * virt * aux_dev, transcendentals=0
        ),
        name=name,
    )(screen, amps, own, *rest)


def own_gamma(own, screen, amps):
    row = jax.ShapeDtypeStruct((1, own.shape[1]), F32)
    part = jax.ShapeDtypeStruct(own.shape, F32)
    masked = jax.ShapeDtypeStruct(own.shape, BF16)
    return gamma_call(own_gamma_kernel, "own_gamma", [masked, part, row], screen, amps, own)


def other_weight(other, screen, amps, weight):
    row = jax.ShapeDtypeStruct((1, other.shape[1]), F32)
    masked = jax.ShapeDtypeStruct(other.shape, BF16)
    return gamma_call(
        other_weight_kernel, "other_weight", [masked, row], screen, amps, other, weight
    )


def gamma_and_virial(own, other, cross, other_cross, part, weight, factor):
    virt, aux_dev = own.shape
    steps = 8 if aux_dev % 1024 == 0 else 1
    vmem = pl.BlockSpec(memory_space=VMEM)
    hbm = pl.BlockSpec(memory_space=pltpu.HBM)
    return pl.pallas_call(
        functools.partial(gamma_kernel, steps),
        in_specs=[vmem] * 7,
        out_specs=[hbm, hbm],
        out_shape=[
            jax.ShapeDtypeStruct((virt, aux_dev), BF16),
            jax.ShapeDtypeStruct((9, aux_dev), F32),
        ],
        scratch_shapes=[
            pltpu.VMEM((virt, aux_dev), BF16),
            pltpu.VMEM((9, aux_dev), F32),
            pltpu.VMEM((virt, virt), BF16),
            pltpu.SemaphoreType.DMA((steps,)),
            pltpu.SemaphoreType.DMA,
        ],
        compiler_params=pltpu.CompilerParams(vmem_limit_bytes=8 << 20),
        cost_estimate=pl.CostEstimate(
            flops=2 * virt * virt * aux_dev, bytes_accessed=8 * virt * aux_dev, transcendentals=0
        ),
        name="gamma_and_virial",
    )(cross, other_cross, own, other, part, weight, factor)


def swap(array, axis, size, bit):
    return lax.ppermute(array, axis, [(i, i ^ bit) for i in range(size)])


def swap_by_core(array, n_aux, bits):
    pairs = [
        (core * n_aux + i, core * n_aux + (i ^ bit))
        for core, bit in enumerate(bits)
        for i in range(n_aux)
    ]
    return lax.ppermute(array, ("occ", "aux"), pairs)


def one_round(total, send, n_aux, bits):
    total = total + swap_by_core(send, n_aux, bits).astype(F32)
    return total, total.astype(BF16)


def after(value, late):
    return lax.optimization_barrier((value, late))


def orders_of(bits):
    if len(bits) != 4:
        turned = bits[1:] + bits[:1]
        return (bits, turned), (bits, turned)
    x, y, z, w = bits
    return ([z, y, x, w], [z, x, w, y]), ([x, y, z, w], [y, z, x, w])


def two_occ_body(n_aux, coeffs, occ_energy, virt_energy, screen, owner, positions):
    raw = coeffs[0]
    other_screen = swap(screen, "occ", 2, 1)
    other_one = swap(occ_energy, "occ", 2, 1)
    other = swap(raw, "occ", 2, 1)
    cross_orders, own_orders = orders_of([1 << k for k in range(n_aux.bit_length() - 1)])
    own, factor, own_sum, own_send = own_pairs(raw, screen, owner, positions)
    cross_sum, cross_send = cross_pairs(own, other, screen, other_screen)
    rounds = len(own_orders[0])
    first_cross = cross_send
    _, other_one = after(first_cross, other_one)
    other_energy = jnp.pad(other_one, (0, LANES - 1))
    for step in range(rounds):
        if step == 1:
            own_send, _ = after(own_send, first_cross)
            cross_send, other_energy = after(cross_send, other_energy)
            energy = swap(other_energy, "occ", 2, 1)
            inverses = inverse_spreads(virt_energy, energy, other_energy)
        if step == max(rounds // 2, 1):
            cross_send, inverses = after(cross_send, inverses)
        own_sum, own_send = one_round(own_sum, own_send, n_aux, [o[step] for o in own_orders])
        cross_sum, cross_send = one_round(
            cross_sum, cross_send, n_aux, [o[step] for o in cross_orders]
        )
    own_inverse, cross_inverse = inverses
    own_amps = (own_sum * own_inverse).astype(BF16)
    own, part, weight = own_gamma(own, screen, own_amps)
    cross = (cross_sum * cross_inverse).astype(BF16)
    cross, part = after(cross, part)
    other_amps = swap(own_amps, "occ", 2, 1)
    other_cross = swap(cross, "occ", 2, 1)
    other, weight = other_weight(other, other_screen, other_amps, weight)
    gamma, virial = gamma_and_virial(own, other, cross, other_cross, part, weight, factor)
    return gamma[None], virial


def general_body(n_aux, coeffs, occ_energy, virt_energy, screen, owner, positions):
    occ_dev, virt, aux_dev = coeffs.shape
    width = aux_dev // screen.shape[1]
    column_mask = jnp.repeat(screen[0], width).astype(BF16)
    masked = coeffs * column_mask[None, None, :]
    whole = lax.all_gather(masked, "occ", axis=0, tiled=True)
    energies = lax.all_gather(occ_energy, "occ", axis=0, tiled=True)
    all_rows = whole.reshape(-1, aux_dev)
    local = masked.reshape(-1, aux_dev)
    virt_f = virt_energy.astype(F32)
    spread_local = (virt_f[None, :] - occ_energy.astype(F32)[:, None]).reshape(-1)
    spread_all = (virt_f[None, :] - energies.astype(F32)[:, None]).reshape(-1)
    pairs = lax.dot_general(all_rows, local, CONTRACT_LAST, preferred_element_type=F32)
    if n_aux & (n_aux - 1):
        summed = lax.psum(pairs, "aux")
    else:
        bits = [1 << k for k in range(n_aux.bit_length() - 1)]
        summed, send = pairs, pairs.astype(BF16)
        for bit in bits:
            summed = summed + swap(send, "aux", n_aux, bit).astype(F32)
            send = summed.astype(BF16)
    amps = (summed / (spread_all[:, None] + spread_local[None, :])).astype(BF16)
    gamma = lax.dot_general(
        amps, all_rows, (((0,), (0,)), ((), ())), preferred_element_type=F32
    ).astype(BF16)
    partial_weight = jnp.sum(gamma.astype(F32) * local.astype(F32), axis=0)
    weight = lax.psum(partial_weight, "occ")
    where = jnp.repeat(positions[:, owner], width, axis=1)
    virial = (where[:, None, :] * where[None, :, :]).reshape(9, aux_dev) * weight[None, :]
    return gamma.reshape(occ_dev, virt, aux_dev), virial


def solution(mesh):
    placed = (P("occ", None, "aux"), P("occ"), P(), P("occ", "aux"), P("aux"), P())
    n_occ, n_aux = mesh.shape["occ"], mesh.shape["aux"]
    power_of_two = n_aux & (n_aux - 1) == 0

    def body(coeffs, *rest):
        even_halves = coeffs.shape[1] % (2 * LANES) == 0
        fits = n_occ == 2 and coeffs.shape[0] == 1 and power_of_two and n_aux > 2 and even_halves
        chosen = two_occ_body if fits else general_body
        return chosen(n_aux, coeffs, *rest)

    return jax.shard_map(
        body,
        mesh=mesh,
        in_specs=placed,
        out_specs=(P("occ", None, "aux"), P(None, "aux")),
        check_vma=False,
    )
```

```python
import functools

import jax
import jax.numpy as jnp
from jax import lax
from jax.experimental import pallas as pl
from jax.experimental.pallas import tpu as pltpu
from jax.sharding import PartitionSpec as P

F32 = jnp.float32
BF16 = jnp.bfloat16
CONTRACT_LAST = (((1,), (1,)), ((), ()))
SMEM = pltpu.MemorySpace.SMEM
VMEM = pltpu.MemorySpace.VMEM
LANES = 128
PAD = 16


def mask_row(screen, first, count, width):
    values = screen.astype(F32)
    pieces = [
        jnp.broadcast_to(values[:, k : k + 1], (1, width)) for k in range(first, first + count)
    ]
    return jnp.concatenate(pieces, axis=1).astype(BF16)


def split(aux_dev, blocks, wanted):
    steps = wanted if blocks % wanted == 0 else 1
    return steps, aux_dev // steps, blocks // steps


def triangle(size):
    return (lax.broadcasted_iota(jnp.int32, (size, size), axis) for axis in (0, 1))


def own_pairs_kernel(
    blocks, width, screen_hbm, owner_hbm, positions_hbm, own_hbm,
    own_ref, factor_ref, sum_ref, send_ref, total, screen, owner, positions, sems,
):
    half = total.shape[0] // 2
    moves = ((screen_hbm, screen), (own_hbm, own_ref), (owner_hbm, owner), (positions_hbm, positions))
    copies = [pltpu.make_async_copy(*move, sems.at[k]) for k, move in enumerate(moves)]
    for copy in copies:
        copy.start()
    copies[0].wait()
    mask = mask_row(screen[...], 0, blocks, width)
    copies[2].wait()
    copies[3].wait()
    for block in range(blocks):
        atom = owner[0, block]
        where = [positions[c, atom] for c in range(3)]
        rows = [
            jnp.full((1, width), where[c] * where[d], F32) for c in range(3) for d in range(3)
        ]
        factor_ref[:, block * width : (block + 1) * width] = jnp.concatenate(rows, axis=0)
    copies[1].wait()
    own = own_ref[...]
    total[...] = lax.dot_general(own * mask, own, CONTRACT_LAST, preferred_element_type=F32)
    low, high = pl.ds(0, half), pl.ds(half, half)
    row, col = triangle(half)
    first, last = total[low, low], total[high, high]
    diagonal = jnp.sum(jnp.where(row == col, last, 0.0), axis=0, keepdims=True)
    parts = (
        total[high, low],
        jnp.where(row >= col, first, last),
        jnp.broadcast_to(diagonal, (PAD, half)),
    )
    start = 0
    for part in parts:
        rows = pl.ds(start, part.shape[0])
        sum_ref[rows, :] = part
        send_ref[rows, :] = part.astype(BF16)
        start += part.shape[0]


def cross_pairs_kernel(
    blocks, width, screen_ref, other_screen_ref, own_ref, other_ref, sum_ref, send_ref, total
):
    half = total.shape[0] // 2
    core = lax.axis_index("occ")
    mask = mask_row(screen_ref[...] * other_screen_ref[...], 0, blocks, width)
    total[...] = lax.dot_general(
        own_ref[...], other_ref[...] * mask, CONTRACT_LAST, preferred_element_type=F32
    )
    for place in range(2):
        rows = pl.ds(place * half, half)
        straight = total[rows, pl.ds(place * half, half)]
        across = total[rows, pl.ds((1 - place) * half, half)]
        part = jnp.where(core == 0, straight, across)
        sum_ref[rows, :] = part
        send_ref[rows, :] = part.astype(BF16)


def in_hbm(array):
    return pltpu.with_memory_space_constraint(array, pltpu.HBM)


def own_pairs(own, screen, owner, positions):
    virt, aux_dev = own.shape
    blocks = screen.shape[1]
    half = virt // 2
    operands = (screen, owner.reshape(1, -1), positions, own)
    return pl.pallas_call(
        functools.partial(own_pairs_kernel, blocks, aux_dev // blocks),
        in_specs=[pl.BlockSpec(memory_space=pltpu.HBM)] * 4,
        out_specs=[pl.BlockSpec(memory_space=VMEM)] * 4,
        out_shape=[
            jax.ShapeDtypeStruct((virt, aux_dev), BF16),
            jax.ShapeDtypeStruct((9, aux_dev), F32),
            jax.ShapeDtypeStruct((2 * half + PAD, half), F32),
            jax.ShapeDtypeStruct((2 * half + PAD, half), BF16),
        ],
        scratch_shapes=[
            pltpu.VMEM((virt, virt), F32),
            pltpu.VMEM((1, blocks), jnp.int32),
            pltpu.SMEM((1, blocks), jnp.int32),
            pltpu.SMEM(positions.shape, F32),
            pltpu.SemaphoreType.DMA((4,)),
        ],
        compiler_params=pltpu.CompilerParams(vmem_limit_bytes=8 << 20),
        cost_estimate=pl.CostEstimate(
            flops=2 * virt * virt * aux_dev, bytes_accessed=2 * virt * aux_dev, transcendentals=0
        ),
        name="own_pairs",
    )(*[in_hbm(operand) for operand in operands])


def cross_pairs(own, other, screen, other_screen):
    virt, aux_dev = own.shape
    blocks = other_screen.shape[1]
    half = virt // 2
    vmem = pl.BlockSpec(memory_space=VMEM)
    return pl.pallas_call(
        functools.partial(cross_pairs_kernel, blocks, aux_dev // blocks),
        in_specs=[vmem] * 4,
        out_specs=[vmem] * 2,
        out_shape=[
            jax.ShapeDtypeStruct((2 * half, half), F32),
            jax.ShapeDtypeStruct((2 * half, half), BF16),
        ],
        scratch_shapes=[pltpu.VMEM((virt, virt), F32)],
        compiler_params=pltpu.CompilerParams(vmem_limit_bytes=8 << 20),
        cost_estimate=pl.CostEstimate(
            flops=8 * virt * virt * aux_dev, bytes_accessed=16 * virt * aux_dev, transcendentals=0
        ),
        name="cross_pairs",
    )(screen, other_screen, own, other)


def symmetric(packed):
    half = packed.shape[1]
    row, col = triangle(half)
    low, both = packed[0:half, :], packed[half : 2 * half, :]
    turned = both.T
    first = jnp.where(row >= col, both, turned)
    last = jnp.where(row < col, both, turned)
    last = jnp.where(row == col, packed[2 * half : 2 * half + 1, :], last)
    top = jnp.concatenate([first, low.T], axis=1)
    return jnp.concatenate([top, jnp.concatenate([low, last], axis=1)], axis=0)


def inverse_kernel(virt_ref, energy_ref, other_energy_ref, own_ref, cross_ref):
    half = own_ref.shape[1]
    energy, other_energy = (
        ref[...].astype(F32)[0:1, 0:1] for ref in (energy_ref, other_energy_ref)
    )
    rows = [
        jnp.broadcast_to(virt_ref[:, k * half : (k + 1) * half].astype(F32), (half, half))
        for k in range(2)
    ]
    cols = [r.T for r in rows]
    row, col = triangle(half)
    twice = [(cols[k] - energy) + (rows[k] - energy) for k in range(2)]
    own_ref[0:half, :] = 1.0 / ((cols[1] - energy) + (rows[0] - energy))
    own_ref[half : 2 * half, :] = 1.0 / jnp.where(row >= col, twice[0], twice[1])
    last = rows[1][0:PAD, :] - energy
    own_ref[2 * half : 2 * half + PAD, :] = 1.0 / (last + last)
    even = lax.axis_index("occ") == 0
    for k in range(2):
        across = jnp.where(even, rows[k], rows[1 - k]) - other_energy
        cross_ref[k * half : (k + 1) * half, :] = 1.0 / ((cols[k] - energy) + across)


def inverse_spreads(virt_energy, energy, other_energy):
    half = virt_energy.shape[0] // 2
    vmem = pl.BlockSpec(memory_space=VMEM)
    return pl.pallas_call(
        inverse_kernel,
        in_specs=[vmem] * 3,
        out_specs=[vmem] * 2,
        out_shape=[
            jax.ShapeDtypeStruct((2 * half + PAD, half), F32),
            jax.ShapeDtypeStruct((2 * half, half), F32),
        ],
        compiler_params=pltpu.CompilerParams(vmem_limit_bytes=4 << 20),
        cost_estimate=pl.CostEstimate(
            flops=32 * half * half, bytes_accessed=32 * half * half, transcendentals=0
        ),
        name="inverse_spreads",
    )(virt_energy.reshape(1, -1), energy.reshape(1, -1), other_energy.reshape(1, -1))


def own_gamma_kernel(
    steps, blocks, width, screen_ref, amps_ref, own_ref, masked_ref, part_ref, weight_ref, amps
):
    tile, per_step = own_ref.shape[1] // steps, blocks // steps
    amps[...] = symmetric(amps_ref[...])
    for step in range(steps):
        columns = pl.ds(step * tile, tile)
        own = own_ref[:, columns] * mask_row(screen_ref[...], step * per_step, per_step, width)
        part = jnp.dot(amps[...], own, preferred_element_type=F32)
        masked_ref[:, columns] = own
        part_ref[:, columns] = part
        weight_ref[:, columns] = jnp.sum(part * own.astype(F32), axis=0, keepdims=True)


def other_weight_kernel(
    steps, blocks, width, screen_ref, amps_ref, own_ref, first_ref, masked_ref, weight_ref, amps
):
    tile, per_step = own_ref.shape[1] // steps, blocks // steps
    amps[...] = symmetric(amps_ref[...])
    for step in range(steps):
        columns = pl.ds(step * tile, tile)
        own = own_ref[:, columns] * mask_row(screen_ref[...], step * per_step, per_step, width)
        part = jnp.dot(amps[...], own, preferred_element_type=F32)
        masked_ref[:, columns] = own
        weight_ref[:, columns] = first_ref[:, columns] + jnp.sum(
            part * own.astype(F32), axis=0, keepdims=True
        )


def gamma_kernel(
    steps, cross_ref, other_cross_ref, own_ref, other_ref, part_ref, weight_ref, factor_ref,
    gamma_hbm, virial_hbm, gamma_ref, virial_ref, amps, sems, virial_sem,
):
    virt, aux_dev = own_ref.shape
    half, tile = virt // 2, aux_dev // steps
    mine = [cross_ref[pl.ds(k * half, half), :] for k in range(2)]
    theirs = [other_cross_ref[pl.ds(k * half, half), :].T for k in range(2)]
    even = lax.axis_index("occ") == 0
    low, high = pl.ds(0, half), pl.ds(half, half)
    amps[low, low] = jnp.where(even, mine[0], theirs[0])
    amps[low, high] = jnp.where(even, theirs[1], mine[0])
    amps[high, low] = jnp.where(even, theirs[0], mine[1])
    amps[high, high] = jnp.where(even, mine[1], theirs[1])
    copies = []
    for step in range(steps):
        columns = pl.ds(step * tile, tile)
        cross = jnp.dot(amps[...], other_ref[:, columns], preferred_element_type=F32)
        gamma_ref[:, columns] = (part_ref[:, columns] + cross).astype(BF16)
        copies.append(
            pltpu.make_async_copy(
                gamma_ref.at[:, columns], gamma_hbm.at[:, columns], sems.at[step]
            )
        )
        copies[step].start()
    for step in range(steps):
        columns = pl.ds(step * tile, tile)
        cross = jnp.dot(amps[...], other_ref[:, columns], preferred_element_type=F32)
        twice = jnp.sum(cross * own_ref[:, columns].astype(F32), axis=0, keepdims=True)
        virial_ref[:, columns] = factor_ref[:, columns] * (weight_ref[:, columns] + 2.0 * twice)
    copies.append(pltpu.make_async_copy(virial_ref, virial_hbm, virial_sem))
    copies[steps].start()
    for copy in copies:
        copy.wait()


def gamma_call(kernel, name, out_shape, screen, amps, own, *rest):
    virt, aux_dev = own.shape
    blocks = screen.shape[1]
    steps = 8 if blocks % 8 == 0 else 1
    vmem = pl.BlockSpec(memory_space=VMEM)
    return pl.pallas_call(
        functools.partial(kernel, steps, blocks, aux_dev // blocks),
        in_specs=[vmem] * (3 + len(rest)),
        out_specs=[vmem] * len(out_shape),
        out_shape=out_shape,
        scratch_shapes=[pltpu.VMEM((virt, virt), BF16)],
        compiler_params=pltpu.CompilerParams(vmem_limit_bytes=8 << 20),
        cost_estimate=pl.CostEstimate(
            flops=2 * virt * virt * aux_dev, bytes_accessed=6 * virt * aux_dev, transcendentals=0
        ),
        name=name,
    )(screen, amps, own, *rest)


def own_gamma(own, screen, amps):
    row = jax.ShapeDtypeStruct((1, own.shape[1]), F32)
    part = jax.ShapeDtypeStruct(own.shape, F32)
    masked = jax.ShapeDtypeStruct(own.shape, BF16)
    return gamma_call(own_gamma_kernel, "own_gamma", [masked, part, row], screen, amps, own)


def other_weight(other, screen, amps, weight):
    row = jax.ShapeDtypeStruct((1, other.shape[1]), F32)
    masked = jax.ShapeDtypeStruct(other.shape, BF16)
    return gamma_call(
        other_weight_kernel, "other_weight", [masked, row], screen, amps, other, weight
    )


def gamma_and_virial(own, other, cross, other_cross, part, weight, factor):
    virt, aux_dev = own.shape
    steps = 8 if aux_dev % 1024 == 0 else 1
    vmem = pl.BlockSpec(memory_space=VMEM)
    hbm = pl.BlockSpec(memory_space=pltpu.HBM)
    return pl.pallas_call(
        functools.partial(gamma_kernel, steps),
        in_specs=[vmem] * 7,
        out_specs=[hbm, hbm],
        out_shape=[
            jax.ShapeDtypeStruct((virt, aux_dev), BF16),
            jax.ShapeDtypeStruct((9, aux_dev), F32),
        ],
        scratch_shapes=[
            pltpu.VMEM((virt, aux_dev), BF16),
            pltpu.VMEM((9, aux_dev), F32),
            pltpu.VMEM((virt, virt), BF16),
            pltpu.SemaphoreType.DMA((steps,)),
            pltpu.SemaphoreType.DMA,
        ],
        compiler_params=pltpu.CompilerParams(vmem_limit_bytes=8 << 20),
        cost_estimate=pl.CostEstimate(
            flops=2 * virt * virt * aux_dev, bytes_accessed=8 * virt * aux_dev, transcendentals=0
        ),
        name="gamma_and_virial",
    )(cross, other_cross, own, other, part, weight, factor)


def swap(array, axis, size, bit):
    return lax.ppermute(array, axis, [(i, i ^ bit) for i in range(size)])


def swap_by_core(array, n_aux, bits):
    pairs = [
        (core * n_aux + i, core * n_aux + (i ^ bit))
        for core, bit in enumerate(bits)
        for i in range(n_aux)
    ]
    return lax.ppermute(array, ("occ", "aux"), pairs)


def one_round(total, send, n_aux, bits):
    total = total + swap_by_core(send, n_aux, bits).astype(F32)
    return total, total.astype(BF16)


def after(value, late):
    return lax.optimization_barrier((value, late))


def orders_of(bits):
    if len(bits) != 4:
        turned = bits[1:] + bits[:1]
        return (bits, turned), (bits, turned)
    x, y, z, w = bits
    return ([z, y, x, w], [z, x, w, y]), ([x, y, z, w], [y, z, x, w])


def two_occ_body(n_aux, coeffs, occ_energy, virt_energy, screen, owner, positions):
    raw = coeffs[0]
    other_screen = swap(screen, "occ", 2, 1)
    other_one = swap(occ_energy, "occ", 2, 1)
    other = swap(raw, "occ", 2, 1)
    cross_orders, own_orders = orders_of([1 << k for k in range(n_aux.bit_length() - 1)])
    own, factor, own_sum, own_send = own_pairs(raw, screen, owner, positions)
    cross_sum, cross_send = cross_pairs(own, other, screen, other_screen)
    rounds = len(own_orders[0])
    first_cross = cross_send
    _, other_one = after(first_cross, other_one)
    other_energy = jnp.pad(other_one, (0, LANES - 1))
    for step in range(rounds):
        if step == 1:
            own_send, _ = after(own_send, first_cross)
            cross_send, other_energy = after(cross_send, other_energy)
            energy = swap(other_energy, "occ", 2, 1)
            inverses = inverse_spreads(virt_energy, energy, other_energy)
        if step == max(rounds // 2, 1):
            cross_send, inverses = after(cross_send, inverses)
        own_sum, own_send = one_round(own_sum, own_send, n_aux, [o[step] for o in own_orders])
        cross_sum, cross_send = one_round(
            cross_sum, cross_send, n_aux, [o[step] for o in cross_orders]
        )
    own_inverse, cross_inverse = inverses
    own_amps = (own_sum * own_inverse).astype(BF16)
    own, part, weight = own_gamma(own, screen, own_amps)
    cross = (cross_sum * cross_inverse).astype(BF16)
    cross, part = after(cross, part)
    other_amps = swap(own_amps, "occ", 2, 1)
    other_cross = swap(cross, "occ", 2, 1)
    other, weight = other_weight(other, other_screen, other_amps, weight)
    gamma, virial = gamma_and_virial(own, other, cross, other_cross, part, weight, factor)
    return gamma[None], virial


def general_body(n_aux, coeffs, occ_energy, virt_energy, screen, owner, positions):
    occ_dev, virt, aux_dev = coeffs.shape
    width = aux_dev // screen.shape[1]
    column_mask = jnp.repeat(screen[0], width).astype(BF16)
    masked = coeffs * column_mask[None, None, :]
    whole = lax.all_gather(masked, "occ", axis=0, tiled=True)
    energies = lax.all_gather(occ_energy, "occ", axis=0, tiled=True)
    all_rows = whole.reshape(-1, aux_dev)
    local = masked.reshape(-1, aux_dev)
    virt_f = virt_energy.astype(F32)
    spread_local = (virt_f[None, :] - occ_energy.astype(F32)[:, None]).reshape(-1)
    spread_all = (virt_f[None, :] - energies.astype(F32)[:, None]).reshape(-1)
    pairs = lax.dot_general(all_rows, local, CONTRACT_LAST, preferred_element_type=F32)
    if n_aux & (n_aux - 1):
        summed = lax.psum(pairs, "aux")
    else:
        bits = [1 << k for k in range(n_aux.bit_length() - 1)]
        summed, send = pairs, pairs.astype(BF16)
        for bit in bits:
            summed = summed + swap(send, "aux", n_aux, bit).astype(F32)
            send = summed.astype(BF16)
    amps = (summed / (spread_all[:, None] + spread_local[None, :])).astype(BF16)
    gamma = lax.dot_general(
        amps, all_rows, (((0,), (0,)), ((), ())), preferred_element_type=F32
    ).astype(BF16)
    partial_weight = jnp.sum(gamma.astype(F32) * local.astype(F32), axis=0)
    weight = lax.psum(partial_weight, "occ")
    where = jnp.repeat(positions[:, owner], width, axis=1)
    virial = (where[:, None, :] * where[None, :, :]).reshape(9, aux_dev) * weight[None, :]
    return gamma.reshape(occ_dev, virt, aux_dev), virial


def solution(mesh):
    placed = (P("occ", None, "aux"), P("occ"), P(), P("occ", "aux"), P("aux"), P())
    n_occ, n_aux = mesh.shape["occ"], mesh.shape["aux"]
    power_of_two = n_aux & (n_aux - 1) == 0

    def body(coeffs, *rest):
        even_halves = coeffs.shape[1] % (2 * LANES) == 0
        fits = n_occ == 2 and coeffs.shape[0] == 1 and power_of_two and n_aux > 2 and even_halves
        chosen = two_occ_body if fits else general_body
        return chosen(n_aux, coeffs, *rest)

    return jax.shard_map(
        body,
        mesh=mesh,
        in_specs=placed,
        out_specs=(P("occ", None, "aux"), P(None, "aux")),
        check_vma=False,
    )
```

```python
import functools

import jax
import jax.numpy as jnp
from jax import lax
from jax.experimental import pallas as pl
from jax.experimental.pallas import tpu as pltpu
from jax.sharding import PartitionSpec as P

F32 = jnp.float32
BF16 = jnp.bfloat16
CONTRACT_LAST = (((1,), (1,)), ((), ()))
SMEM = pltpu.MemorySpace.SMEM
VMEM = pltpu.MemorySpace.VMEM
LANES = 128
PAD = 16


def mask_row(screen, first, count, width):
    values = screen.astype(F32)
    pieces = [
        jnp.broadcast_to(values[:, k : k + 1], (1, width)) for k in range(first, first + count)
    ]
    return jnp.concatenate(pieces, axis=1).astype(BF16)


def split(aux_dev, blocks, wanted):
    steps = wanted if blocks % wanted == 0 else 1
    return steps, aux_dev // steps, blocks // steps


def triangle(size):
    return (lax.broadcasted_iota(jnp.int32, (size, size), axis) for axis in (0, 1))


def own_pairs_kernel(
    blocks, width, screen_hbm, owner_hbm, positions_hbm, own_hbm,
    own_ref, factor_ref, sum_ref, send_ref, total, screen, owner, positions, sems,
):
    half = total.shape[0] // 2
    moves = ((screen_hbm, screen), (own_hbm, own_ref), (owner_hbm, owner), (positions_hbm, positions))
    copies = [pltpu.make_async_copy(*move, sems.at[k]) for k, move in enumerate(moves)]
    for copy in copies:
        copy.start()
    copies[0].wait()
    mask = mask_row(screen[...], 0, blocks, width)
    copies[2].wait()
    copies[3].wait()
    for block in range(blocks):
        atom = owner[0, block]
        where = [positions[c, atom] for c in range(3)]
        rows = [
            jnp.full((1, width), where[c] * where[d], F32) for c in range(3) for d in range(3)
        ]
        factor_ref[:, block * width : (block + 1) * width] = jnp.concatenate(rows, axis=0)
    copies[1].wait()
    own = own_ref[...]
    total[...] = lax.dot_general(own * mask, own, CONTRACT_LAST, preferred_element_type=F32)
    low, high = pl.ds(0, half), pl.ds(half, half)
    row, col = triangle(half)
    first, last = total[low, low], total[high, high]
    diagonal = jnp.sum(jnp.where(row == col, last, 0.0), axis=0, keepdims=True)
    parts = (
        total[high, low],
        jnp.where(row >= col, first, last),
        jnp.broadcast_to(diagonal, (PAD, half)),
    )
    start = 0
    for part in parts:
        rows = pl.ds(start, part.shape[0])
        sum_ref[rows, :] = part
        send_ref[rows, :] = part.astype(BF16)
        start += part.shape[0]


def cross_pairs_kernel(
    blocks, width, screen_ref, other_screen_ref, own_ref, other_ref, sum_ref, send_ref, total
):
    half = total.shape[0] // 2
    core = lax.axis_index("occ")
    mask = mask_row(screen_ref[...] * other_screen_ref[...], 0, blocks, width)
    total[...] = lax.dot_general(
        own_ref[...], other_ref[...] * mask, CONTRACT_LAST, preferred_element_type=F32
    )
    for place in range(2):
        rows = pl.ds(place * half, half)
        straight = total[rows, pl.ds(place * half, half)]
        across = total[rows, pl.ds((1 - place) * half, half)]
        part = jnp.where(core == 0, straight, across)
        sum_ref[rows, :] = part
        send_ref[rows, :] = part.astype(BF16)


def in_hbm(array):
    return pltpu.with_memory_space_constraint(array, pltpu.HBM)


def own_pairs(own, screen, owner, positions):
    virt, aux_dev = own.shape
    blocks = screen.shape[1]
    half = virt // 2
    operands = (screen, owner.reshape(1, -1), positions, own)
    return pl.pallas_call(
        functools.partial(own_pairs_kernel, blocks, aux_dev // blocks),
        in_specs=[pl.BlockSpec(memory_space=pltpu.HBM)] * 4,
        out_specs=[pl.BlockSpec(memory_space=VMEM)] * 4,
        out_shape=[
            jax.ShapeDtypeStruct((virt, aux_dev), BF16),
            jax.ShapeDtypeStruct((9, aux_dev), F32),
            jax.ShapeDtypeStruct((2 * half + PAD, half), F32),
            jax.ShapeDtypeStruct((2 * half + PAD, half), BF16),
        ],
        scratch_shapes=[
            pltpu.VMEM((virt, virt), F32),
            pltpu.VMEM((1, blocks), jnp.int32),
            pltpu.SMEM((1, blocks), jnp.int32),
            pltpu.SMEM(positions.shape, F32),
            pltpu.SemaphoreType.DMA((4,)),
        ],
        compiler_params=pltpu.CompilerParams(vmem_limit_bytes=8 << 20),
        cost_estimate=pl.CostEstimate(
            flops=2 * virt * virt * aux_dev, bytes_accessed=2 * virt * aux_dev, transcendentals=0
        ),
        name="own_pairs",
    )(*[in_hbm(operand) for operand in operands])


def cross_pairs(own, other, screen, other_screen):
    virt, aux_dev = own.shape
    blocks = other_screen.shape[1]
    half = virt // 2
    vmem = pl.BlockSpec(memory_space=VMEM)
    return pl.pallas_call(
        functools.partial(cross_pairs_kernel, blocks, aux_dev // blocks),
        in_specs=[vmem] * 4,
        out_specs=[vmem] * 2,
        out_shape=[
            jax.ShapeDtypeStruct((2 * half, half), F32),
            jax.ShapeDtypeStruct((2 * half, half), BF16),
        ],
        scratch_shapes=[pltpu.VMEM((virt, virt), F32)],
        compiler_params=pltpu.CompilerParams(vmem_limit_bytes=8 << 20),
        cost_estimate=pl.CostEstimate(
            flops=8 * virt * virt * aux_dev, bytes_accessed=16 * virt * aux_dev, transcendentals=0
        ),
        name="cross_pairs",
    )(screen, other_screen, own, other)


def symmetric(packed):
    half = packed.shape[1]
    row, col = triangle(half)
    low, both = packed[0:half, :], packed[half : 2 * half, :]
    turned = both.T
    first = jnp.where(row >= col, both, turned)
    last = jnp.where(row < col, both, turned)
    last = jnp.where(row == col, packed[2 * half : 2 * half + 1, :], last)
    top = jnp.concatenate([first, low.T], axis=1)
    return jnp.concatenate([top, jnp.concatenate([low, last], axis=1)], axis=0)


def inverse_kernel(virt_ref, energy_ref, other_energy_ref, own_ref, cross_ref):
    half = own_ref.shape[1]
    energy, other_energy = (
        ref[...].astype(F32)[0:1, 0:1] for ref in (energy_ref, other_energy_ref)
    )
    rows = [
        jnp.broadcast_to(virt_ref[:, k * half : (k + 1) * half].astype(F32), (half, half))
        for k in range(2)
    ]
    cols = [r.T for r in rows]
    row, col = triangle(half)
    twice = [(cols[k] - energy) + (rows[k] - energy) for k in range(2)]
    own_ref[0:half, :] = 1.0 / ((cols[1] - energy) + (rows[0] - energy))
    own_ref[half : 2 * half, :] = 1.0 / jnp.where(row >= col, twice[0], twice[1])
    last = rows[1][0:PAD, :] - energy
    own_ref[2 * half : 2 * half + PAD, :] = 1.0 / (last + last)
    even = lax.axis_index("occ") == 0
    for k in range(2):
        across = jnp.where(even, rows[k], rows[1 - k]) - other_energy
        cross_ref[k * half : (k + 1) * half, :] = 1.0 / ((cols[k] - energy) + across)


def inverse_spreads(virt_energy, energy, other_energy):
    half = virt_energy.shape[0] // 2
    vmem = pl.BlockSpec(memory_space=VMEM)
    return pl.pallas_call(
        inverse_kernel,
        in_specs=[vmem] * 3,
        out_specs=[vmem] * 2,
        out_shape=[
            jax.ShapeDtypeStruct((2 * half + PAD, half), F32),
            jax.ShapeDtypeStruct((2 * half, half), F32),
        ],
        compiler_params=pltpu.CompilerParams(vmem_limit_bytes=4 << 20),
        cost_estimate=pl.CostEstimate(
            flops=32 * half * half, bytes_accessed=32 * half * half, transcendentals=0
        ),
        name="inverse_spreads",
    )(virt_energy.reshape(1, -1), energy.reshape(1, -1), other_energy.reshape(1, -1))


def own_gamma_kernel(
    steps, blocks, width, screen_ref, amps_ref, own_ref, masked_ref, part_ref, weight_ref, amps
):
    tile, per_step = own_ref.shape[1] // steps, blocks // steps
    amps[...] = symmetric(amps_ref[...])
    for step in range(steps):
        columns = pl.ds(step * tile, tile)
        own = own_ref[:, columns] * mask_row(screen_ref[...], step * per_step, per_step, width)
        part = jnp.dot(amps[...], own, preferred_element_type=F32)
        masked_ref[:, columns] = own
        part_ref[:, columns] = part
        weight_ref[:, columns] = jnp.sum(part * own.astype(F32), axis=0, keepdims=True)


def other_weight_kernel(
    steps, blocks, width, screen_ref, amps_ref, own_ref, first_ref, masked_ref, weight_ref, amps
):
    tile, per_step = own_ref.shape[1] // steps, blocks // steps
    amps[...] = symmetric(amps_ref[...])
    for step in range(steps):
        columns = pl.ds(step * tile, tile)
        own = own_ref[:, columns] * mask_row(screen_ref[...], step * per_step, per_step, width)
        part = jnp.dot(amps[...], own, preferred_element_type=F32)
        masked_ref[:, columns] = own
        weight_ref[:, columns] = first_ref[:, columns] + jnp.sum(
            part * own.astype(F32), axis=0, keepdims=True
        )


def gamma_kernel(
    steps, cross_ref, other_cross_ref, own_ref, other_ref, part_ref, weight_ref, factor_ref,
    gamma_hbm, virial_hbm, gamma_ref, virial_ref, amps, sems, virial_sem,
):
    virt, aux_dev = own_ref.shape
    half, tile = virt // 2, aux_dev // steps
    mine = [cross_ref[pl.ds(k * half, half), :] for k in range(2)]
    theirs = [other_cross_ref[pl.ds(k * half, half), :].T for k in range(2)]
    even = lax.axis_index("occ") == 0
    low, high = pl.ds(0, half), pl.ds(half, half)
    amps[low, low] = jnp.where(even, mine[0], theirs[0])
    amps[low, high] = jnp.where(even, theirs[1], mine[0])
    amps[high, low] = jnp.where(even, theirs[0], mine[1])
    amps[high, high] = jnp.where(even, mine[1], theirs[1])
    copies = []
    for step in range(steps):
        columns = pl.ds(step * tile, tile)
        cross = jnp.dot(amps[...], other_ref[:, columns], preferred_element_type=F32)
        gamma_ref[:, columns] = (part_ref[:, columns] + cross).astype(BF16)
        copies.append(
            pltpu.make_async_copy(
                gamma_ref.at[:, columns], gamma_hbm.at[:, columns], sems.at[step]
            )
        )
        copies[step].start()
        twice = jnp.sum(cross * own_ref[:, columns].astype(F32), axis=0, keepdims=True)
        virial_ref[:, columns] = factor_ref[:, columns] * (weight_ref[:, columns] + 2.0 * twice)
    copies.append(pltpu.make_async_copy(virial_ref, virial_hbm, virial_sem))
    copies[steps].start()
    for copy in copies:
        copy.wait()


def gamma_call(kernel, name, out_shape, screen, amps, own, *rest):
    virt, aux_dev = own.shape
    blocks = screen.shape[1]
    steps = 8 if blocks % 8 == 0 else 1
    vmem = pl.BlockSpec(memory_space=VMEM)
    return pl.pallas_call(
        functools.partial(kernel, steps, blocks, aux_dev // blocks),
        in_specs=[vmem] * (3 + len(rest)),
        out_specs=[vmem] * len(out_shape),
        out_shape=out_shape,
        scratch_shapes=[pltpu.VMEM((virt, virt), BF16)],
        compiler_params=pltpu.CompilerParams(vmem_limit_bytes=8 << 20),
        cost_estimate=pl.CostEstimate(
            flops=2 * virt * virt * aux_dev, bytes_accessed=6 * virt * aux_dev, transcendentals=0
        ),
        name=name,
    )(screen, amps, own, *rest)


def own_gamma(own, screen, amps):
    row = jax.ShapeDtypeStruct((1, own.shape[1]), F32)
    part = jax.ShapeDtypeStruct(own.shape, F32)
    masked = jax.ShapeDtypeStruct(own.shape, BF16)
    return gamma_call(own_gamma_kernel, "own_gamma", [masked, part, row], screen, amps, own)


def other_weight(other, screen, amps, weight):
    row = jax.ShapeDtypeStruct((1, other.shape[1]), F32)
    masked = jax.ShapeDtypeStruct(other.shape, BF16)
    return gamma_call(
        other_weight_kernel, "other_weight", [masked, row], screen, amps, other, weight
    )


def gamma_and_virial(own, other, cross, other_cross, part, weight, factor):
    virt, aux_dev = own.shape
    steps = 8 if aux_dev % 1024 == 0 else 1
    vmem = pl.BlockSpec(memory_space=VMEM)
    hbm = pl.BlockSpec(memory_space=pltpu.HBM)
    return pl.pallas_call(
        functools.partial(gamma_kernel, steps),
        in_specs=[vmem] * 7,
        out_specs=[hbm, hbm],
        out_shape=[
            jax.ShapeDtypeStruct((virt, aux_dev), BF16),
            jax.ShapeDtypeStruct((9, aux_dev), F32),
        ],
        scratch_shapes=[
            pltpu.VMEM((virt, aux_dev), BF16),
            pltpu.VMEM((9, aux_dev), F32),
            pltpu.VMEM((virt, virt), BF16),
            pltpu.SemaphoreType.DMA((steps,)),
            pltpu.SemaphoreType.DMA,
        ],
        compiler_params=pltpu.CompilerParams(vmem_limit_bytes=8 << 20),
        cost_estimate=pl.CostEstimate(
            flops=2 * virt * virt * aux_dev, bytes_accessed=8 * virt * aux_dev, transcendentals=0
        ),
        name="gamma_and_virial",
    )(cross, other_cross, own, other, part, weight, factor)


def swap(array, axis, size, bit):
    return lax.ppermute(array, axis, [(i, i ^ bit) for i in range(size)])


def swap_by_core(array, n_aux, bits):
    pairs = [
        (core * n_aux + i, core * n_aux + (i ^ bit))
        for core, bit in enumerate(bits)
        for i in range(n_aux)
    ]
    return lax.ppermute(array, ("occ", "aux"), pairs)


def one_round(total, send, n_aux, bits):
    total = total + swap_by_core(send, n_aux, bits).astype(F32)
    return total, total.astype(BF16)


def after(value, late):
    return lax.optimization_barrier((value, late))


def orders_of(bits):
    if len(bits) != 4:
        turned = bits[1:] + bits[:1]
        return (bits, turned), (bits, turned)
    x, y, z, w = bits
    return ([x, y, z, w], [z, x, w, y]), ([x, y, z, w], [w, z, x, y])


def two_occ_body(n_aux, coeffs, occ_energy, virt_energy, screen, owner, positions):
    raw = coeffs[0]
    other_screen = swap(screen, "occ", 2, 1)
    other_one = swap(occ_energy, "occ", 2, 1)
    other = swap(raw, "occ", 2, 1)
    cross_orders, own_orders = orders_of([1 << k for k in range(n_aux.bit_length() - 1)])
    own, factor, own_sum, own_send = own_pairs(raw, screen, owner, positions)
    cross_sum, cross_send = cross_pairs(own, other, screen, other_screen)
    rounds = len(own_orders[0])
    first_cross = cross_send
    _, other_one = after(first_cross, other_one)
    other_energy = jnp.pad(other_one, (0, LANES - 1))
    for step in range(rounds):
        if step == 1:
            own_send, _ = after(own_send, first_cross)
            cross_send, other_energy = after(cross_send, other_energy)
            energy = swap(other_energy, "occ", 2, 1)
            inverses = inverse_spreads(virt_energy, energy, other_energy)
        if step == max(rounds // 2, 1):
            cross_send, inverses = after(cross_send, inverses)
        own_sum, own_send = one_round(own_sum, own_send, n_aux, [o[step] for o in own_orders])
        cross_sum, cross_send = one_round(
            cross_sum, cross_send, n_aux, [o[step] for o in cross_orders]
        )
    own_inverse, cross_inverse = inverses
    own_amps = (own_sum * own_inverse).astype(BF16)
    own, part, weight = own_gamma(own, screen, own_amps)
    cross = (cross_sum * cross_inverse).astype(BF16)
    cross, part = after(cross, part)
    other_amps = swap(own_amps, "occ", 2, 1)
    other_cross = swap(cross, "occ", 2, 1)
    other, weight = other_weight(other, other_screen, other_amps, weight)
    gamma, virial = gamma_and_virial(own, other, cross, other_cross, part, weight, factor)
    return gamma[None], virial


def general_body(n_aux, coeffs, occ_energy, virt_energy, screen, owner, positions):
    occ_dev, virt, aux_dev = coeffs.shape
    width = aux_dev // screen.shape[1]
    column_mask = jnp.repeat(screen[0], width).astype(BF16)
    masked = coeffs * column_mask[None, None, :]
    whole = lax.all_gather(masked, "occ", axis=0, tiled=True)
    energies = lax.all_gather(occ_energy, "occ", axis=0, tiled=True)
    all_rows = whole.reshape(-1, aux_dev)
    local = masked.reshape(-1, aux_dev)
    virt_f = virt_energy.astype(F32)
    spread_local = (virt_f[None, :] - occ_energy.astype(F32)[:, None]).reshape(-1)
    spread_all = (virt_f[None, :] - energies.astype(F32)[:, None]).reshape(-1)
    pairs = lax.dot_general(all_rows, local, CONTRACT_LAST, preferred_element_type=F32)
    if n_aux & (n_aux - 1):
        summed = lax.psum(pairs, "aux")
    else:
        bits = [1 << k for k in range(n_aux.bit_length() - 1)]
        summed, send = pairs, pairs.astype(BF16)
        for bit in bits:
            summed = summed + swap(send, "aux", n_aux, bit).astype(F32)
            send = summed.astype(BF16)
    amps = (summed / (spread_all[:, None] + spread_local[None, :])).astype(BF16)
    gamma = lax.dot_general(
        amps, all_rows, (((0,), (0,)), ((), ())), preferred_element_type=F32
    ).astype(BF16)
    partial_weight = jnp.sum(gamma.astype(F32) * local.astype(F32), axis=0)
    weight = lax.psum(partial_weight, "occ")
    where = jnp.repeat(positions[:, owner], width, axis=1)
    virial = (where[:, None, :] * where[None, :, :]).reshape(9, aux_dev) * weight[None, :]
    return gamma.reshape(occ_dev, virt, aux_dev), virial


def solution(mesh):
    placed = (P("occ", None, "aux"), P("occ"), P(), P("occ", "aux"), P("aux"), P())
    n_occ, n_aux = mesh.shape["occ"], mesh.shape["aux"]
    power_of_two = n_aux & (n_aux - 1) == 0

    def body(coeffs, *rest):
        even_halves = coeffs.shape[1] % (2 * LANES) == 0
        fits = n_occ == 2 and coeffs.shape[0] == 1 and power_of_two and n_aux > 2 and even_halves
        chosen = two_occ_body if fits else general_body
        return chosen(n_aux, coeffs, *rest)

    return jax.shard_map(
        body,
        mesh=mesh,
        in_specs=placed,
        out_specs=(P("occ", None, "aux"), P(None, "aux")),
        check_vma=False,
    )
```
